512 devices in a mesh: island: 16 (over z, core), shard: 32 (over x, y).
Axes of the slice: x: 4, y: 8, z: 8, core: 2. Of those that a mesh axis runs over, the one named last changes fastest.
Arguments:
- island_deltas: bfloat16 [16, 12288, 4096], P('island', 'shard'), may hold values from -192 to 192
- start_basis: bfloat16 [4096, 128], P('shard'), may hold values from -6 to 6
- outer_params: float32 [12288, 4096], P('shard', 'island'), may hold values from -6 to 6
- momentum: float32 [12288, 4096], P('shard', 'island'), may hold values from -3 to 3
Outputs:
- new_params: float32 [12288, 4096], P('shard', 'island')
- new_momentum: float32 [12288, 4096], P('shard', 'island')
The draws below stay inside these ranges and needn't reach their ends.
All inputs are finite; a program needn't handle non-finite values.
Results may differ from the reference program's by a relative error of at most 0.0013.
Values may be sent and summed in bfloat16 or wider, within the bound.
A program may use at most 64 MiB of HBM per device.

```python
import jax
import jax.numpy as jnp
from jax import lax

N = 4096
R = 128
M = 12288
N_ISLAND = 16


def spiked(entries, stream_key, source, target, shards_of, factor):
    def block_of(axis_at):
        return (jnp.arange(entries.shape[axis_at]) // (entries.shape[axis_at] // shards_of)).reshape((-1,) + (1,) * (entries.ndim - 1 - axis_at))

    first = jax.random.permutation(stream_key, shards_of)[block_of(target)]
    second = (block_of(target) + shards_of // 2) % shards_of
    return jnp.where((block_of(source) == first) | (block_of(source) == second), factor * entries, entries)


def level_of(rng, extent, split, least, largest):
    gain, own = 1.0, jax.random.fold_in(rng, 6)
    for axis_at, blocks in split:
        steps = jnp.exp(jax.random.uniform(jax.random.fold_in(own, axis_at), (blocks,), jnp.float32, least / len(split), largest / len(split)))
        gain = gain * jnp.repeat(steps, extent[axis_at] // blocks).reshape([-1 if axis == axis_at else 1 for axis in range(len(extent))])
    return gain


def noise(rng, dims, scale, limit, shards=(), kind=jnp.bfloat16):
    array = jax.random.normal(rng, dims, jnp.float32) * scale
    if len(shards) > 0:
        array = level_of(rng, dims, shards, -0.22, 0.18) * array
    return jnp.clip(array, min=-limit, max=limit).astype(kind)


def heavy_noise(own_key, shape, spread, limit, split, heavy, held_as=jnp.bfloat16):
    values = spread * jax.random.normal(own_key, shape, jnp.float32)
    if split:
        values = values * level_of(own_key, shape, split, -0.22, 0.18)
    return jnp.clip(spiked(values, jax.random.fold_in(own_key, 3), *heavy), -limit, limit).astype(held_as)


def setup_inputs(seed: int = 0) -> dict:
    streams_of = jax.random.split(jax.random.key(seed), 5)
    return {
        "island_deltas": heavy_noise(streams_of[0], (N_ISLAND, M, N), 16.0, 192.0, ((0, 16), (1, 32)), (1, 2, 32, 2.75)),
        "start_basis": noise(streams_of[1], (N, R), 1.0, 6.0, ((0, 32),)),
        "outer_params": noise(streams_of[2], (M, N), 1.0, 6.0, ((0, 32), (1, 16)), jnp.float32),
        "momentum": noise(streams_of[3], (M, N), 0.5, 3.0, ((0, 32), (1, 16)), jnp.float32),
    }


outer_rate = 0.7
outer_decay = 0.9

def reference(island_deltas, start_basis, outer_params, momentum):
    rows = island_deltas.shape[1]
    rank = start_basis.shape[1]
    width = island_deltas.shape[2]

    def add_left(total, delta):
        return (total + jnp.dot(delta.astype(jnp.float32), start_basis.astype(jnp.float32), preferred_element_type=jnp.float32), None)
    left_total, unused = lax.scan(add_left, jnp.zeros((rows, rank), jnp.float32), island_deltas)
    left = left_total / N_ISLAND
    gram = jnp.dot(left.T, left, precision=lax.Precision.HIGHEST)
    factor = jnp.linalg.cholesky(gram)
    ortho = lax.linalg.triangular_solve(factor, left, left_side=False, lower=True, transpose_a=True)
    ortho_bf = ortho.astype(jnp.bfloat16)

    def add_right(total, delta):
        term = lax.dot_general(delta.astype(jnp.float32), ortho_bf.astype(jnp.float32), (((0,), (0,)), ((), ())), preferred_element_type=jnp.float32)
        return (total + term, None)
    right_total, unused = lax.scan(add_right, jnp.zeros((width, rank), jnp.float32), island_deltas)
    right = right_total / N_ISLAND
    grad = jnp.dot(ortho, right.T, precision=lax.Precision.HIGHEST)
    new_momentum = outer_decay * momentum + grad
    new_params = outer_params - outer_rate * (grad + outer_decay * new_momentum)
    return (new_params, new_momentum)
```

```python
import functools

import jax
import jax.numpy as jnp
from jax import lax
from jax.experimental import pallas as pl
from jax.experimental.pallas import tpu as pltpu
from jax.sharding import PartitionSpec as P

outer_rate = 0.7
outer_decay = 0.9

MESH = pl.DeviceIdType.MESH
F32 = jnp.float32
BF16 = jnp.bfloat16
HIGHEST = lax.Precision.HIGHEST

NX, NY, NZ = 4, 8, 8
ROWS = 384
RANK = 128
HALF = ROWS // 2
PIECE = HALF // NZ
BLOCK = 256
SHARD = 128
SLICE = RANK // NX


def dot(a, b, precision=None):
    return jnp.dot(a, b, preferred_element_type=F32, precision=precision)


def invert_steps(a, steps):
    lane = lax.broadcasted_iota(jnp.int32, (8, RANK), 1)
    row = lax.broadcasted_iota(jnp.int32, (8, RANK), 0)

    def step(_, a):
        panel = a[0:8, :]
        columns = [jnp.broadcast_to(panel[:, j : j + 1], (8, RANK)) for j in range(8)]
        panel = jnp.where(lane < 8, (lane == row).astype(F32), panel)
        for j in range(8):
            here = row == j
            pivot = 1.0 / jnp.broadcast_to(columns[j][j : j + 1, :], (8, RANK))

            def reduced(values, j=j, here=here, pivot=pivot):
                scaled = jnp.broadcast_to(values[j : j + 1, :], (8, RANK)) * pivot
                return jnp.where(here, scaled, values - columns[j] * scaled)

            panel = reduced(panel)
            for m in range(j + 1, 8):
                columns[m] = reduced(columns[m])
        rest = a[8:, :]
        kept = jnp.where(lax.broadcasted_iota(jnp.int32, rest.shape, 1) < 8, 0.0, rest)
        for j in range(8):
            kept = kept - jnp.broadcast_to(rest[:, j : j + 1], rest.shape) * jnp.broadcast_to(
                panel[j : j + 1, :], rest.shape
            )
        return pltpu.roll(jnp.concatenate([kept, panel], axis=0), RANK - 8, 1)

    return lax.fori_loop(0, steps, step, a)


def kernel(
    deltas, basis, params, momentum,
    new_params, new_momentum,
    d_own, d_sib, s_all, l_part, l_sib, l_half, l_in, l_all,
    r_f32, r_b16, r_x, r_z, r_zin, r_y, r_yin, r_all,
    g_own, g_yin, g_x, g_xin, g_all, p_v, m_v, np_v, nm_v,
    local_sem,
    ds_s, ds_r, sy_s, sy_r, sx_s, sx_r, lc_s, lc_r, lz_s, lz_r, la_s, la_r, lf_s, lf_r,
    rx_s, rx_r, rz_s, rz_r, ry_s, ry_r, ra_s, ra_r, gy_s, gy_r, gx_s, gx_r, gc_s, gc_r,
):
    island = lax.axis_index("island")
    shard = lax.axis_index("shard")
    z, c = island // 2, lax.rem(island, 2)
    x, y = shard // NY, lax.rem(shard, NY)
    o = 1 - c

    def at_x(d):
        return (island, lax.rem(x + d, NX) * NY + y)

    def at_y(d):
        return (island, x * NY + lax.rem(y + d, NY))

    def at_z(d):
        return (lax.rem(z + d, NZ) * 2 + c, shard)

    sibling = (z * 2 + o, shard)
    sends = []

    def send(src, dst, s, r, device):
        copy = pltpu.make_async_remote_copy(
            src_ref=src, dst_ref=dst, send_sem=s, recv_sem=r, device_id=device, device_id_type=MESH
        )
        copy.start()
        sends.append(copy)

    def arrive(dst, s, r):
        pltpu.make_async_remote_copy(
            src_ref=dst, dst_ref=dst, send_sem=s, recv_sem=r, device_id=sibling, device_id_type=MESH
        ).wait_recv()

    barrier = pltpu.get_barrier_semaphore()
    partners = [at_y(d) for d in range(1, NY)] + [at_z(d) for d in range(1, NZ)] + [at_x(d) for d in range(1, NX)]
    for device in partners + [sibling]:
        pl.semaphore_signal(barrier, inc=1, device_id=device, device_id_type=MESH)

    loads = []
    for b in range(NZ):
        cols = pl.ds(pl.multiple_of((2 * b + c) * BLOCK, BLOCK), BLOCK)
        loads.append(pltpu.make_async_copy(deltas.at[0, :, cols], d_own.at[:, pl.ds(b * BLOCK, BLOCK)], local_sem.at[b]))
    state = [
        pltpu.make_async_copy(params, p_v, local_sem.at[NZ]),
        pltpu.make_async_copy(momentum, m_v, local_sem.at[NZ + 1]),
    ]
    for copy in loads + state:
        copy.start()

    pl.semaphore_wait(barrier, len(partners) + 1)

    mine = lax.rem(y // 2, 2) == c
    own_slot = 4 * x + 2 * (y // 4) + lax.rem(y, 2)

    def slot(index):
        return s_all.at[pl.ds(pl.multiple_of(index * SHARD, SHARD), SHARD)]

    def y_copies():
        own_k = own_slot - 4 * x
        return [
            pltpu.make_async_remote_copy(
                src_ref=basis, dst_ref=slot(own_slot), send_sem=sy_s.at[d], recv_sem=sy_r.at[own_k],
                device_id=at_y(d), device_id_type=MESH,
            )
            for d in range(1, NY)
        ]

    @pl.when(mine)
    def _():
        for copy in y_copies():
            copy.start()
        here = pltpu.make_async_copy(basis, slot(own_slot), local_sem.at[NZ + 2])
        here.start()
        here.wait()

    for b in range(NZ):
        cols = pl.ds(pl.multiple_of((2 * b + o) * BLOCK, BLOCK), BLOCK)
        send(deltas.at[0, :, cols], d_sib.at[:, pl.ds(b * BLOCK, BLOCK)], ds_s.at[b], ds_r.at[b], sibling)

    for k in range(4):
        source = (k % 2) + 2 * c + 4 * (k // 2)

        @pl.when(source != y)
        def _(k=k):
            arrive(slot(4 * x + k), sy_s.at[0], sy_r.at[k])

        for d in range(1, NX):
            send(slot(4 * x + k), slot(4 * x + k), sx_s.at[d, k], sx_r.at[d, k], at_x(d))
    for d in range(1, NX):
        for k in range(4):
            arrive(slot(4 * lax.rem(x + NX - d, NX) + k), sx_s.at[d, k], sx_r.at[d, k])
    for b in range(NZ):
        loads[b].wait()
        arrive(d_sib.at[:, pl.ds(b * BLOCK, BLOCK)], ds_s.at[b], ds_r.at[b])

    l_part[...] = dot(d_own[...], s_all[...]) + dot(d_sib[...], s_all[...])
    send(l_part.at[pl.ds(pl.multiple_of(HALF * o, HALF), HALF)], l_sib, lc_s.at[0], lc_r.at[0], sibling)
    arrive(l_sib, lc_s.at[0], lc_r.at[0])
    l_half[...] = l_part[pl.ds(pl.multiple_of(HALF * c, HALF), HALF), :] + l_sib[...]
    for d in range(1, NZ):
        rows = pl.ds(pl.multiple_of(PIECE * lax.rem(z + d, NZ), 8), PIECE)
        send(l_half.at[rows], l_in.at[d], lz_s.at[d], lz_r.at[d], at_z(d))
    total = l_half[pl.ds(pl.multiple_of(PIECE * z, 8), PIECE), :]
    for d in range(1, NZ):
        arrive(l_in.at[d], lz_s.at[d], lz_r.at[d])
        total = total + l_in[d]

    def piece(d):
        return pl.ds(pl.multiple_of(HALF * c + PIECE * lax.rem(z + NZ - d, NZ), 8), PIECE)

    def sibling_piece(d):
        return pl.ds(pl.multiple_of(HALF * o + PIECE * lax.rem(z + NZ - d, NZ), 8), PIECE)

    l_all[piece(0), :] = total
    for d in range(1, NZ):
        send(l_all.at[piece(0)], l_all.at[piece(0)], la_s.at[d], la_r.at[d], at_z(d))
    for d in range(NZ):
        if d:
            arrive(l_all.at[piece(d)], la_s.at[d], la_r.at[d])
        send(l_all.at[piece(d)], l_all.at[piece(d)], lf_s.at[d], lf_r.at[d], sibling)
    for d in range(NZ):
        arrive(l_all.at[sibling_piece(d)], lf_s.at[d], lf_r.at[d])

    left = l_all[...]
    left_t = left.T
    g_part = dot(left_t, left, HIGHEST)
    g_own[...] = jnp.where(c == 0, g_part[: RANK // 2], g_part[RANK // 2 :])
    for d in range(1, NY):
        send(g_own, g_yin.at[d], gy_s.at[d], gy_r.at[d], at_y(d))

    high = left_t.astype(BF16)
    low = (left_t - high.astype(F32)).astype(BF16)
    both = jnp.concatenate([high, low], axis=0)
    for b in range(NZ):
        cols = slice(b * BLOCK, (b + 1) * BLOCK)
        term = dot(both, d_own[:, cols]) + dot(both, d_sib[:, cols])
        term = term[:RANK] + term[RANK:]
        r_f32[b] = term
        r_b16[b] = term.astype(BF16)
        if b % 4 == 3:
            h = b // 4
            for d in range(1, NX):
                rank = pl.ds(pl.multiple_of(SLICE * lax.rem(x + d, NX), SLICE), SLICE)
                send(
                    r_b16.at[pl.ds(4 * h, 4), rank], r_x.at[d, pl.ds(4 * h, 4)],
                    rx_s.at[d, h], rx_r.at[d, h], at_x(d),
                )

    gram = g_own[...]
    for d in range(1, NY):
        arrive(g_yin.at[d], gy_s.at[d], gy_r.at[d])
        gram = gram + g_yin[d]
    g_x[...] = gram
    for d in range(1, NX):
        send(g_x, g_xin.at[d], gx_s.at[d], gx_r.at[d], at_x(d))

    rank_x = pl.ds(pl.multiple_of(SLICE * x, SLICE), SLICE)
    for h in range(2):
        for d in range(1, NX):
            arrive(r_x.at[d, pl.ds(4 * h, 4)], rx_s.at[d, h], rx_r.at[d, h])
        for b in range(4 * h, 4 * h + 4):
            term = r_f32[b, rank_x, :]
            for d in range(1, NX):
                term = term + r_x[d, b].astype(F32)
            r_z[b] = term
    for d in range(1, NZ):
        send(r_z.at[lax.rem(z + d, NZ)], r_zin.at[d], rz_s.at[d], rz_r.at[d], at_z(d))

    for d in range(1, NX):
        arrive(g_xin.at[d], gx_s.at[d], gx_r.at[d])
        gram = gram + g_xin[d]
    rows_c = pl.ds(pl.multiple_of(RANK // 2 * c, RANK // 2), RANK // 2)
    rows_o = pl.ds(pl.multiple_of(RANK // 2 * o, RANK // 2), RANK // 2)
    g_all[rows_c, :] = gram
    send(g_all.at[rows_c], g_all.at[rows_c], gc_s.at[0], gc_r.at[0], sibling)
    arrive(g_all.at[rows_o], gc_s.at[0], gc_r.at[0])
    inverse = invert_steps(g_all[...], 6)

    term = r_z[z]
    for d in range(1, NZ):
        arrive(r_zin.at[d], rz_s.at[d], rz_r.at[d])
        term = term + r_zin[d]
    r_y[...] = term
    for d in range(1, NY):
        send(r_y, r_yin.at[d], ry_s.at[d], ry_r.at[d], at_y(d))
    inverse = invert_steps(inverse, 10)
    ortho = dot(l_all[...], inverse, HIGHEST) * (1.0 / 16.0)
    for d in range(1, NY):
        arrive(r_yin.at[d], ry_s.at[d], ry_r.at[d])
        term = term + r_yin[d]
    r_all[rank_x, :] = term
    for d in range(1, NX):
        send(r_all.at[rank_x], r_all.at[rank_x], ra_s.at[d], ra_r.at[d], at_x(d))
    for copy in state:
        copy.wait()
    for d in range(1, NX):
        rank = pl.ds(pl.multiple_of(SLICE * lax.rem(x + NX - d, NX), SLICE), SLICE)
        arrive(r_all.at[rank], ra_s.at[d], ra_r.at[d])

    grad = dot(ortho, r_all[...], HIGHEST)
    updated = outer_decay * m_v[...] + grad
    nm_v[...] = updated
    np_v[...] = p_v[...] - outer_rate * (grad + outer_decay * updated)
    stores = [
        pltpu.make_async_copy(np_v, new_params, local_sem.at[NZ + 3]),
        pltpu.make_async_copy(nm_v, new_momentum, local_sem.at[NZ + 4]),
    ]
    for copy in stores:
        copy.start()
    for copy in sends:
        copy.wait_send()

    @pl.when(mine)
    def _():
        for copy in y_copies():
            copy.wait_send()

    for copy in stores:
        copy.wait()


def body(island_deltas, start_basis, outer_params, momentum):
    dma = pltpu.SemaphoreType.DMA
    vmem = pltpu.VMEM
    pair = lambda *shape: [dma(shape), dma(shape)]
    scratch = [
        vmem((ROWS, NZ * BLOCK), BF16),
        vmem((ROWS, NZ * BLOCK), BF16),
        vmem((NZ * BLOCK, RANK), BF16),
        vmem((ROWS, RANK), F32),
        vmem((HALF, RANK), F32),
        vmem((HALF, RANK), F32),
        vmem((NZ, PIECE, RANK), F32),
        vmem((ROWS, RANK), F32),
        vmem((NZ, RANK, BLOCK), F32),
        vmem((NZ, RANK, BLOCK), BF16),
        vmem((NX, NZ, SLICE, BLOCK), BF16),
        vmem((NZ, SLICE, BLOCK), F32),
        vmem((NZ, SLICE, BLOCK), F32),
        vmem((SLICE, BLOCK), F32),
        vmem((NY, SLICE, BLOCK), F32),
        vmem((RANK, BLOCK), F32),
        vmem((RANK // 2, RANK), F32),
        vmem((NY, RANK // 2, RANK), F32),
        vmem((RANK // 2, RANK), F32),
        vmem((NX, RANK // 2, RANK), F32),
        vmem((RANK, RANK), F32),
        vmem((ROWS, BLOCK), F32),
        vmem((ROWS, BLOCK), F32),
        vmem((ROWS, BLOCK), F32),
        vmem((ROWS, BLOCK), F32),
        dma((NZ + 5,)),
        *pair(NZ),
        dma((NY,)),
        dma((4,)),
        *pair(NX, 4),
        *pair(1),
        *pair(NZ),
        *pair(NZ),
        *pair(NZ),
        *pair(NX, 2),
        *pair(NZ),
        *pair(NY),
        *pair(NX),
        *pair(NY),
        *pair(NX),
        *pair(1),
    ]
    state = jax.ShapeDtypeStruct(outer_params.shape, F32)
    return tuple(
        pl.pallas_call(
            kernel,
            name="outer_step",
            out_shape=(state, state),
            in_specs=[pl.BlockSpec(memory_space=pl.ANY), pl.BlockSpec(memory_space=pltpu.VMEM)]
            + [pl.BlockSpec(memory_space=pl.ANY)] * 2,
            out_specs=(pl.BlockSpec(memory_space=pl.ANY),) * 2,
            scratch_shapes=scratch,
            compiler_params=pltpu.CompilerParams(
                collective_id=0, has_side_effects=True, vmem_limit_bytes=58 * 1024 * 1024
            ),
        )(island_deltas, start_basis, outer_params, momentum)
    )


def solution(mesh):
    placed = (
        P("island", "shard", None),
        P("shard", None),
        P("shard", "island"),
        P("shard", "island"),
    )
    return jax.shard_map(
        body,
        mesh=mesh,
        in_specs=placed,
        out_specs=(P("shard", "island"), P("shard", "island")),
        check_vma=False,
    )
```

```python
import functools

import jax
import jax.numpy as jnp
from jax import lax
from jax.experimental import pallas as pl
from jax.experimental.pallas import tpu as pltpu
from jax.sharding import PartitionSpec as P

outer_rate = 0.7
outer_decay = 0.9

MESH = pl.DeviceIdType.MESH
F32 = jnp.float32
BF16 = jnp.bfloat16
HIGHEST = lax.Precision.HIGHEST

NX, NY, NZ = 4, 8, 8
ROWS = 384
RANK = 128
HALF = ROWS // 2
PIECE = HALF // NZ
BLOCK = 256
SHARD = 128
SLICE = RANK // NX


AROUND_8 = (4, 3, 5, 2, 6, 1, 7)
AROUND_4 = (2, 1, 3)


def dot(a, b, precision=None):
    return jnp.dot(a, b, preferred_element_type=F32, precision=precision)


def invert_steps(a, steps):
    lane = lax.broadcasted_iota(jnp.int32, (8, RANK), 1)
    row = lax.broadcasted_iota(jnp.int32, (8, RANK), 0)

    def step(_, a):
        panel = a[0:8, :]
        columns = [jnp.broadcast_to(panel[:, j : j + 1], (8, RANK)) for j in range(8)]
        panel = jnp.where(lane < 8, (lane == row).astype(F32), panel)
        for j in range(8):
            here = row == j
            pivot = 1.0 / jnp.broadcast_to(columns[j][j : j + 1, :], (8, RANK))

            def reduced(values, j=j, here=here, pivot=pivot):
                scaled = jnp.broadcast_to(values[j : j + 1, :], (8, RANK)) * pivot
                return jnp.where(here, scaled, values - columns[j] * scaled)

            panel = reduced(panel)
            for m in range(j + 1, 8):
                columns[m] = reduced(columns[m])
        rest = a[8:, :]
        kept = jnp.where(lax.broadcasted_iota(jnp.int32, rest.shape, 1) < 8, 0.0, rest)
        for j in range(8):
            kept = kept - jnp.broadcast_to(rest[:, j : j + 1], rest.shape) * jnp.broadcast_to(
                panel[j : j + 1, :], rest.shape
            )
        return pltpu.roll(jnp.concatenate([kept, panel], axis=0), RANK - 8, 1)

    return lax.fori_loop(0, steps, step, a)


def kernel(
    deltas, basis, grad_out,
    d_own, d_sib, s_all, l_part, l_sib, l_half, l_in, l_all,
    a_f32, a_b16, a_x, a_z, a_zin, b_f32, b_b16, b_zin, b_x, b_xin, r_y, r_yin, r_all,
    g_own, g_yin, g_x, g_xin, g_all,
    local_sem,
    ds_s, ds_r, sy_s, sy_r, sx_s, sx_r, lc_s, lc_r, lz_s, lz_r, la_s, la_r, lf_s, lf_r,
    ax_s, ax_r, az_s, az_r, bz_s, bz_r, bx_s, bx_r, ry_s, ry_r, ra_s, ra_r, gy_s, gy_r, gx_s, gx_r, gc_s, gc_r,
):
    island = lax.axis_index("island")
    shard = lax.axis_index("shard")
    z, c = island // 2, lax.rem(island, 2)
    x, y = shard // NY, lax.rem(shard, NY)
    o = 1 - c

    def at_x(d):
        return (island, lax.rem(x + d, NX) * NY + y)

    def at_y(d):
        return (island, x * NY + lax.rem(y + d, NY))

    def at_z(d):
        return (lax.rem(z + d, NZ) * 2 + c, shard)

    sibling = (z * 2 + o, shard)
    sends = []

    def send(src, dst, s, r, device):
        copy = pltpu.make_async_remote_copy(
            src_ref=src, dst_ref=dst, send_sem=s, recv_sem=r, device_id=device, device_id_type=MESH
        )
        copy.start()
        sends.append(copy)

    def arrive(dst, s, r):
        pltpu.make_async_remote_copy(
            src_ref=dst, dst_ref=dst, send_sem=s, recv_sem=r, device_id=sibling, device_id_type=MESH
        ).wait_recv()

    barrier = pltpu.get_barrier_semaphore()
    partners = [at_y(d) for d in range(1, NY)] + [at_z(d) for d in range(1, NZ)] + [at_x(d) for d in range(1, NX)]
    for device in partners + [sibling]:
        pl.semaphore_signal(barrier, inc=1, device_id=device, device_id_type=MESH)

    loads = []
    for b in range(NZ):
        cols = pl.ds(pl.multiple_of((2 * b + c) * BLOCK, BLOCK), BLOCK)
        loads.append(pltpu.make_async_copy(deltas.at[0, :, cols], d_own.at[:, pl.ds(b * BLOCK, BLOCK)], local_sem.at[b]))
    for copy in loads:
        copy.start()

    pl.semaphore_wait(barrier, len(partners) + 1)

    mine = lax.rem(y // 2, 2) == c
    own_slot = 4 * x + 2 * (y // 4) + lax.rem(y, 2)

    def slot(index):
        return s_all.at[pl.ds(pl.multiple_of(index * SHARD, SHARD), SHARD)]

    def y_copies():
        own_k = own_slot - 4 * x
        return [
            pltpu.make_async_remote_copy(
                src_ref=basis, dst_ref=slot(own_slot), send_sem=sy_s.at[d], recv_sem=sy_r.at[own_k],
                device_id=at_y(d), device_id_type=MESH,
            )
            for d in AROUND_8
        ]

    @pl.when(mine)
    def _():
        for copy in y_copies():
            copy.start()
        here = pltpu.make_async_copy(basis, slot(own_slot), local_sem.at[NZ])
        here.start()
        here.wait()

    for b in range(NZ):
        cols = pl.ds(pl.multiple_of((2 * b + o) * BLOCK, BLOCK), BLOCK)
        send(deltas.at[0, :, cols], d_sib.at[:, pl.ds(b * BLOCK, BLOCK)], ds_s.at[b], ds_r.at[b], sibling)

    turn = 1 - 2 * lax.rem(y, 2)
    order = [jnp.where(mine, a, b) * turn for a, b in ((0, -1), (1, 2), (-3, -2), (4, 3))]
    for n, offset in enumerate(order):
        source = lax.rem(y + offset + NY, NY)
        k = lax.rem(source, 2) + 2 * (source // 4)
        if n == 0:

            @pl.when(jnp.logical_not(mine))
            def _():
                arrive(slot(4 * x + k), sy_s.at[0], sy_r.at[k])
        else:
            arrive(slot(4 * x + k), sy_s.at[0], sy_r.at[k])
        for d in AROUND_4:
            send(slot(4 * x + k), slot(4 * x + k), sx_s.at[d, n], sx_r.at[d, k], at_x(d))

    for b in range(NZ):
        loads[b].wait()
        arrive(d_sib.at[:, pl.ds(b * BLOCK, BLOCK)], ds_s.at[b], ds_r.at[b])

    def left_term(d):
        quarter = pl.ds(pl.multiple_of(4 * SHARD * lax.rem(x + NX - d, NX), 4 * SHARD), 4 * SHARD)
        return dot(d_own[:, quarter], s_all[quarter, :]) + dot(d_sib[:, quarter], s_all[quarter, :])

    l_part[...] = left_term(0)
    for d in (1, 3, 2):
        for k in range(4):
            arrive(slot(4 * lax.rem(x + NX - d, NX) + k), sx_s.at[d, k], sx_r.at[d, k])
        l_part[...] += left_term(d)
    send(l_part.at[pl.ds(pl.multiple_of(HALF * o, HALF), HALF)], l_sib, lc_s.at[0], lc_r.at[0], sibling)
    arrive(l_sib, lc_s.at[0], lc_r.at[0])
    l_half[...] = l_part[pl.ds(pl.multiple_of(HALF * c, HALF), HALF), :] + l_sib[...]
    for d in AROUND_8:
        rows = pl.ds(pl.multiple_of(PIECE * lax.rem(z + d, NZ), 8), PIECE)
        send(l_half.at[rows], l_in.at[d], lz_s.at[d], lz_r.at[d], at_z(d))
    total = l_half[pl.ds(pl.multiple_of(PIECE * z, 8), PIECE), :]
    for d in range(1, NZ):
        arrive(l_in.at[d], lz_s.at[d], lz_r.at[d])
        total = total + l_in[d]

    def piece(d):
        return pl.ds(pl.multiple_of(HALF * c + PIECE * lax.rem(z + NZ - d, NZ), 8), PIECE)

    def sibling_piece(d):
        return pl.ds(pl.multiple_of(HALF * o + PIECE * lax.rem(z + NZ - d, NZ), 8), PIECE)

    l_all[piece(0), :] = total
    for d in AROUND_8:
        send(l_all.at[piece(0)], l_all.at[piece(0)], la_s.at[d], la_r.at[d], at_z(d))
    for d in (0, *reversed(AROUND_8)):
        if d:
            arrive(l_all.at[piece(d)], la_s.at[d], la_r.at[d])
        send(l_all.at[piece(d)], l_all.at[piece(d)], lf_s.at[d], lf_r.at[d], sibling)
    for d in range(NZ):
        arrive(l_all.at[sibling_piece(d)], lf_s.at[d], lf_r.at[d])

    left = l_all[...]
    left_t = left.T
    high = left_t.astype(BF16)
    low = (left_t - high.astype(F32)).astype(BF16)
    both = jnp.concatenate([high, low], axis=0)

    def rank_of(d):
        return pl.ds(pl.multiple_of(SLICE * lax.rem(x + d, NX), SLICE), SLICE)

    for n, away in enumerate((*AROUND_8, 0)):
        cols = pl.ds(pl.multiple_of(BLOCK * lax.rem(z + away, NZ), BLOCK), BLOCK)
        term = dot(both, d_own[:, cols]) + dot(both, d_sib[:, cols])
        term = term[:RANK] + term[RANK:]
        a_f32[n] = term[:, :RANK]
        a_b16[n] = term[:, :RANK].astype(BF16)
        if away:
            b_b16[n] = term[:, RANK:].astype(BF16)
            send(b_b16.at[n], b_zin.at[n], bz_s.at[n], bz_r.at[n], at_z(away))
        else:
            b_f32[...] = term[:, RANK:]
        if n % 4 == 3:
            h = n // 4
            part = pl.ds(4 * h, 4)
            for d in AROUND_4:
                send(a_b16.at[part, rank_of(d)], a_x.at[d, part], ax_s.at[d, h], ax_r.at[d, h], at_x(d))

    g_part = dot(left_t, left, HIGHEST)
    g_own[...] = jnp.where(c == 0, g_part[: RANK // 2], g_part[RANK // 2 :])
    for d in AROUND_8:
        send(g_own, g_yin.at[d], gy_s.at[d], gy_r.at[d], at_y(d))

    for h in range(2):
        for d in range(1, NX):
            arrive(a_x.at[d, pl.ds(4 * h, 4)], ax_s.at[d, h], ax_r.at[d, h])
        for n in range(4 * h, 4 * h + 4):
            term = a_f32[n, rank_of(0), :]
            for d in range(1, NX):
                term = term + a_x[d, n].astype(F32)
            a_z[n] = term
            if n < NZ - 1:
                send(a_z.at[n], a_zin.at[n], az_s.at[n], az_r.at[n], at_z(AROUND_8[n]))

    b_sum = b_f32[...]
    for n in range(NZ - 1):
        arrive(b_zin.at[n], bz_s.at[n], bz_r.at[n])
        b_sum = b_sum + b_zin[n].astype(F32)
    b_x[...] = b_sum
    for d in AROUND_4:
        send(b_x.at[rank_of(d)], b_xin.at[d], bx_s.at[d], bx_r.at[d], at_x(d))

    gram = g_own[...]
    for d in range(1, NY):
        arrive(g_yin.at[d], gy_s.at[d], gy_r.at[d])
        gram = gram + g_yin[d]
    g_x[...] = gram
    for d in AROUND_4:
        send(g_x, g_xin.at[d], gx_s.at[d], gx_r.at[d], at_x(d))

    a_sum = a_z[NZ - 1]
    for n in range(NZ - 1):
        arrive(a_zin.at[n], az_s.at[n], az_r.at[n])
        a_sum = a_sum + a_zin[n]
    b_sum = b_x[rank_of(0), :]
    for d in range(1, NX):
        arrive(b_xin.at[d], bx_s.at[d], bx_r.at[d])
        b_sum = b_sum + b_xin[d]
    r_y[0] = a_sum
    r_y[1] = b_sum
    for d in AROUND_8:
        send(r_y, r_yin.at[d], ry_s.at[d], ry_r.at[d], at_y(d))

    for d in range(1, NX):
        arrive(g_xin.at[d], gx_s.at[d], gx_r.at[d])
        gram = gram + g_xin[d]
    rows_c = pl.ds(pl.multiple_of(RANK // 2 * c, RANK // 2), RANK // 2)
    rows_o = pl.ds(pl.multiple_of(RANK // 2 * o, RANK // 2), RANK // 2)
    g_all[rows_c, :] = gram
    send(g_all.at[rows_c], g_all.at[rows_c], gc_s.at[0], gc_r.at[0], sibling)
    arrive(g_all.at[rows_o], gc_s.at[0], gc_r.at[0])
    inverse = invert_steps(g_all[...], 10)

    term = r_y[...]
    for d in range(1, NY):
        arrive(r_yin.at[d], ry_s.at[d], ry_r.at[d])
        term = term + r_yin[d]
    r_all[:, rank_of(0), :] = term
    for d in AROUND_4:
        send(r_all.at[:, rank_of(0)], r_all.at[:, rank_of(0)], ra_s.at[d], ra_r.at[d], at_x(d))
    inverse = invert_steps(inverse, 6)
    ortho = dot(l_all[...], inverse, HIGHEST) * (1.0 / 16.0)
    for d in range(1, NX):
        arrive(r_all.at[:, rank_of(NX - d)], ra_s.at[d], ra_r.at[d])
    for h in range(2):
        grad_out[:, h * RANK : (h + 1) * RANK] = dot(ortho, r_all[h], HIGHEST)

    for copy in sends:
        copy.wait_send()

    @pl.when(mine)
    def _():
        for copy in y_copies():
            copy.wait_send()


def body(island_deltas, start_basis, outer_params, momentum):
    dma = pltpu.SemaphoreType.DMA
    vmem = pltpu.VMEM
    pair = lambda *shape: [dma(shape), dma(shape)]
    scratch = [
        vmem((ROWS, NZ * BLOCK), BF16),
        vmem((ROWS, NZ * BLOCK), BF16),
        vmem((NZ * BLOCK, RANK), BF16),
        vmem((ROWS, RANK), F32),
        vmem((HALF, RANK), F32),
        vmem((HALF, RANK), F32),
        vmem((NZ, PIECE, RANK), F32),
        vmem((ROWS, RANK), F32),
        vmem((NZ, RANK, RANK), F32),
        vmem((NZ, RANK, RANK), BF16),
        vmem((NX, NZ, SLICE, RANK), BF16),
        vmem((NZ, SLICE, RANK), F32),
        vmem((NZ, SLICE, RANK), F32),
        vmem((RANK, RANK), F32),
        vmem((NZ, RANK, RANK), BF16),
        vmem((NZ, RANK, RANK), BF16),
        vmem((RANK, RANK), F32),
        vmem((NX, SLICE, RANK), F32),
        vmem((2, SLICE, RANK), F32),
        vmem((NY, 2, SLICE, RANK), F32),
        vmem((2, RANK, RANK), F32),
        vmem((RANK // 2, RANK), F32),
        vmem((NY, RANK // 2, RANK), F32),
        vmem((RANK // 2, RANK), F32),
        vmem((NX, RANK // 2, RANK), F32),
        vmem((RANK, RANK), F32),
        dma((NZ + 1,)),
        *pair(NZ),
        dma((NY,)),
        dma((4,)),
        *pair(NX, 4),
        *pair(1),
        *pair(NZ),
        *pair(NZ),
        *pair(NZ),
        *pair(NX, 2),
        *pair(NZ),
        *pair(NZ),
        *pair(NX),
        *pair(NY),
        *pair(NX),
        *pair(NY),
        *pair(NX),
        *pair(1),
    ]
    grad = pl.pallas_call(
        kernel,
        name="outer_step",
        out_shape=jax.ShapeDtypeStruct(outer_params.shape, F32),
        in_specs=[pl.BlockSpec(memory_space=pltpu.HBM), pl.BlockSpec(memory_space=pltpu.VMEM)],
        out_specs=pl.BlockSpec(memory_space=pltpu.VMEM),
        scratch_shapes=scratch,
        compiler_params=pltpu.CompilerParams(
            collective_id=0, has_side_effects=True, vmem_limit_bytes=60 * 1024 * 1024
        ),
    )(island_deltas, start_basis)
    new_momentum = outer_decay * momentum + grad
    new_params = outer_params - outer_rate * (grad + outer_decay * new_momentum)
    return (new_params, new_momentum)


def solution(mesh):
    placed = (
        P("island", "shard", None),
        P("shard", None),
        P("shard", "island"),
        P("shard", "island"),
    )
    return jax.shard_map(
        body,
        mesh=mesh,
        in_specs=placed,
        out_specs=(P("shard", "island"), P("shard", "island")),
        check_vma=False,
    )
```

```python
import functools

import jax
import jax.numpy as jnp
from jax import lax
from jax.experimental import pallas as pl
from jax.experimental.pallas import tpu as pltpu
from jax.sharding import PartitionSpec as P

outer_rate = 0.7
outer_decay = 0.9

MESH = pl.DeviceIdType.MESH
F32 = jnp.float32
BF16 = jnp.bfloat16
HIGHEST = lax.Precision.HIGHEST

NX, NY, NZ = 4, 8, 8
ROWS = 384
RANK = 128
HALF = ROWS // 2
PIECE = HALF // NZ
BLOCK = 256
SHARD = 128
SLICE = RANK // NX


AROUND_8 = (4, 3, 5, 2, 6, 1, 7)
AROUND_4 = (2, 1, 3)


def dot(a, b, precision=None):
    return jnp.dot(a, b, preferred_element_type=F32, precision=precision)


def invert_steps(a, steps):
    lane = lax.broadcasted_iota(jnp.int32, (8, RANK), 1)
    row = lax.broadcasted_iota(jnp.int32, (8, RANK), 0)

    def step(_, a):
        panel = a[0:8, :]
        columns = [jnp.broadcast_to(panel[:, j : j + 1], (8, RANK)) for j in range(8)]
        panel = jnp.where(lane < 8, (lane == row).astype(F32), panel)
        for j in range(8):
            here = row == j
            pivot = 1.0 / jnp.broadcast_to(columns[j][j : j + 1, :], (8, RANK))

            def reduced(values, j=j, here=here, pivot=pivot):
                scaled = jnp.broadcast_to(values[j : j + 1, :], (8, RANK)) * pivot
                return jnp.where(here, scaled, values - columns[j] * scaled)

            panel = reduced(panel)
            for m in range(j + 1, 8):
                columns[m] = reduced(columns[m])
        rest = a[8:, :]
        kept = jnp.where(lax.broadcasted_iota(jnp.int32, rest.shape, 1) < 8, 0.0, rest)
        for j in range(8):
            kept = kept - jnp.broadcast_to(rest[:, j : j + 1], rest.shape) * jnp.broadcast_to(
                panel[j : j + 1, :], rest.shape
            )
        return pltpu.roll(jnp.concatenate([kept, panel], axis=0), RANK - 8, 1)

    return lax.fori_loop(0, steps, step, a)


def kernel(
    deltas, basis, ortho_out, r_all,
    basis_v, d_own, d_sib, s_all, l_part, l_sib, l_half, l_in, l_all,
    a_f32, a_b16, a_x, a_z, a_zin, b_f32, b_b16, b_zin, b_x, b_xin, r_y, r_yin,
    g_own, g_yin, g_x, g_xin, g_all,
    local_sem,
    ds_s, ds_r, sy_s, sy_r, sx_s, sx_r, lc_s, lc_r, lz_s, lz_r, la_s, la_r, lf_s, lf_r,
    ax_s, ax_r, az_s, az_r, bz_s, bz_r, bx_s, bx_r, ry_s, ry_r, ra_s, ra_r, gy_s, gy_r, gx_s, gx_r, gc_s, gc_r,
):
    island = lax.axis_index("island")
    shard = lax.axis_index("shard")
    z, c = island // 2, lax.rem(island, 2)
    x, y = shard // NY, lax.rem(shard, NY)
    o = 1 - c

    def at_x(d):
        return (island, lax.rem(x + d, NX) * NY + y)

    def at_y(d):
        return (island, x * NY + lax.rem(y + d, NY))

    def at_z(d):
        return (lax.rem(z + d, NZ) * 2 + c, shard)

    sibling = (z * 2 + o, shard)
    sends = []

    def send(src, dst, s, r, device):
        copy = pltpu.make_async_remote_copy(
            src_ref=src, dst_ref=dst, send_sem=s, recv_sem=r, device_id=device, device_id_type=MESH
        )
        copy.start()
        sends.append(copy)

    def arrive(dst, s, r):
        pltpu.make_async_remote_copy(
            src_ref=dst, dst_ref=dst, send_sem=s, recv_sem=r, device_id=sibling, device_id_type=MESH
        ).wait_recv()

    barrier = pltpu.get_barrier_semaphore()
    partners = [at_y(d) for d in range(1, NY)] + [at_z(d) for d in range(1, NZ)] + [at_x(d) for d in range(1, NX)]
    for device in partners + [sibling]:
        pl.semaphore_signal(barrier, inc=1, device_id=device, device_id_type=MESH)

    basis_load = pltpu.make_async_copy(basis, basis_v, local_sem.at[NZ])
    basis_load.start()
    loads = []
    for b in range(NZ):
        cols = pl.ds(pl.multiple_of((2 * b + c) * BLOCK, BLOCK), BLOCK)
        loads.append(pltpu.make_async_copy(deltas.at[0, :, cols], d_own.at[:, pl.ds(b * BLOCK, BLOCK)], local_sem.at[b]))
    for copy in loads:
        copy.start()

    basis_load.wait()
    pl.semaphore_wait(barrier, len(partners) + 1)

    mine = lax.rem(y // 2, 2) == c
    own_slot = 4 * x + 2 * (y // 4) + lax.rem(y, 2)

    def slot(index):
        return s_all.at[pl.ds(pl.multiple_of(index * SHARD, SHARD), SHARD)]

    def y_copies():
        own_k = own_slot - 4 * x
        return [
            pltpu.make_async_remote_copy(
                src_ref=basis_v, dst_ref=slot(own_slot), send_sem=sy_s.at[d], recv_sem=sy_r.at[own_k],
                device_id=at_y(d), device_id_type=MESH,
            )
            for d in AROUND_8
        ]

    @pl.when(mine)
    def _():
        for copy in y_copies():
            copy.start()
        slot(own_slot)[...] = basis_v[...]

    for b in range(NZ):
        cols = pl.ds(pl.multiple_of((2 * b + o) * BLOCK, BLOCK), BLOCK)
        send(deltas.at[0, :, cols], d_sib.at[:, pl.ds(b * BLOCK, BLOCK)], ds_s.at[b], ds_r.at[b], sibling)

    turn = 1 - 2 * lax.rem(y, 2)
    order = [jnp.where(mine, a, b) * turn for a, b in ((0, -1), (1, 2), (-3, -2), (4, 3))]
    for n, offset in enumerate(order):
        source = lax.rem(y + offset + NY, NY)
        k = lax.rem(source, 2) + 2 * (source // 4)
        if n == 0:

            @pl.when(jnp.logical_not(mine))
            def _():
                arrive(slot(4 * x + k), sy_s.at[0], sy_r.at[k])
        else:
            arrive(slot(4 * x + k), sy_s.at[0], sy_r.at[k])
        for d in AROUND_4:
            send(slot(4 * x + k), slot(4 * x + k), sx_s.at[d, n], sx_r.at[d, k], at_x(d))

    for b in range(NZ):
        loads[b].wait()
        arrive(d_sib.at[:, pl.ds(b * BLOCK, BLOCK)], ds_s.at[b], ds_r.at[b])

    def left_term(d):
        quarter = pl.ds(pl.multiple_of(4 * SHARD * lax.rem(x + NX - d, NX), 4 * SHARD), 4 * SHARD)
        return dot(d_own[:, quarter], s_all[quarter, :]) + dot(d_sib[:, quarter], s_all[quarter, :])

    l_part[...] = left_term(0)
    for d in (1, 3, 2):
        for k in range(4):
            arrive(slot(4 * lax.rem(x + NX - d, NX) + k), sx_s.at[d, k], sx_r.at[d, k])
        l_part[...] += left_term(d)
    send(l_part.at[pl.ds(pl.multiple_of(HALF * o, HALF), HALF)], l_sib, lc_s.at[0], lc_r.at[0], sibling)
    arrive(l_sib, lc_s.at[0], lc_r.at[0])
    l_half[...] = l_part[pl.ds(pl.multiple_of(HALF * c, HALF), HALF), :] + l_sib[...]
    for d in AROUND_8:
        rows = pl.ds(pl.multiple_of(PIECE * lax.rem(z + d, NZ), 8), PIECE)
        send(l_half.at[rows], l_in.at[d], lz_s.at[d], lz_r.at[d], at_z(d))
    total = l_half[pl.ds(pl.multiple_of(PIECE * z, 8), PIECE), :]
    for d in range(1, NZ):
        arrive(l_in.at[d], lz_s.at[d], lz_r.at[d])
        total = total + l_in[d]

    def piece(d):
        return pl.ds(pl.multiple_of(HALF * c + PIECE * lax.rem(z + NZ - d, NZ), 8), PIECE)

    def sibling_piece(d):
        return pl.ds(pl.multiple_of(HALF * o + PIECE * lax.rem(z + NZ - d, NZ), 8), PIECE)

    l_all[piece(0), :] = total
    for d in AROUND_8:
        send(l_all.at[piece(0)], l_all.at[piece(0)], la_s.at[d], la_r.at[d], at_z(d))
    for d in (0, *reversed(AROUND_8)):
        if d:
            arrive(l_all.at[piece(d)], la_s.at[d], la_r.at[d])
        send(l_all.at[piece(d)], l_all.at[piece(d)], lf_s.at[d], lf_r.at[d], sibling)
    for d in range(NZ):
        arrive(l_all.at[sibling_piece(d)], lf_s.at[d], lf_r.at[d])

    left = l_all[...]
    left_t = left.T
    high = left_t.astype(BF16)
    low = (left_t - high.astype(F32)).astype(BF16)
    both = jnp.concatenate([high, low], axis=0)

    def rank_of(d):
        return pl.ds(pl.multiple_of(SLICE * lax.rem(x + d, NX), SLICE), SLICE)

    for n, away in enumerate((*AROUND_8, 0)):
        cols = pl.ds(pl.multiple_of(BLOCK * lax.rem(z + away, NZ), BLOCK), BLOCK)
        term = dot(both, d_own[:, cols]) + dot(both, d_sib[:, cols])
        term = term[:RANK] + term[RANK:]
        a_f32[n] = term[:, :RANK]
        a_b16[n] = term[:, :RANK].astype(BF16)
        if away:
            b_b16[n] = term[:, RANK:].astype(BF16)
            send(b_b16.at[n], b_zin.at[n], bz_s.at[n], bz_r.at[n], at_z(away))
        else:
            b_f32[...] = term[:, RANK:]
        if n % 4 == 3:
            h = n // 4
            part = pl.ds(4 * h, 4)
            for d in AROUND_4:
                send(a_b16.at[part, rank_of(d)], a_x.at[d, part], ax_s.at[d, h], ax_r.at[d, h], at_x(d))

    g_part = dot(left_t, left, HIGHEST)
    g_own[...] = jnp.where(c == 0, g_part[: RANK // 2], g_part[RANK // 2 :])
    for d in AROUND_8:
        send(g_own, g_yin.at[d], gy_s.at[d], gy_r.at[d], at_y(d))

    for h in range(2):
        for d in range(1, NX):
            arrive(a_x.at[d, pl.ds(4 * h, 4)], ax_s.at[d, h], ax_r.at[d, h])
        for n in range(4 * h, 4 * h + 4):
            term = a_f32[n, rank_of(0), :]
            for d in range(1, NX):
                term = term + a_x[d, n].astype(F32)
            a_z[n] = term
            if n < NZ - 1:
                send(a_z.at[n], a_zin.at[n], az_s.at[n], az_r.at[n], at_z(AROUND_8[n]))

    b_sum = b_f32[...]
    for n in range(NZ - 1):
        arrive(b_zin.at[n], bz_s.at[n], bz_r.at[n])
        b_sum = b_sum + b_zin[n].astype(F32)
    b_x[...] = b_sum
    for d in AROUND_4:
        send(b_x.at[rank_of(d)], b_xin.at[d], bx_s.at[d], bx_r.at[d], at_x(d))

    gram = g_own[...]
    for d in range(1, NY):
        arrive(g_yin.at[d], gy_s.at[d], gy_r.at[d])
        gram = gram + g_yin[d]
    g_x[...] = gram
    for d in AROUND_4:
        send(g_x, g_xin.at[d], gx_s.at[d], gx_r.at[d], at_x(d))

    a_sum = a_z[NZ - 1]
    for n in range(NZ - 1):
        arrive(a_zin.at[n], az_s.at[n], az_r.at[n])
        a_sum = a_sum + a_zin[n]
    b_sum = b_x[rank_of(0), :]
    for d in range(1, NX):
        arrive(b_xin.at[d], bx_s.at[d], bx_r.at[d])
        b_sum = b_sum + b_xin[d]
    r_y[0] = a_sum
    r_y[1] = b_sum
    for d in AROUND_8:
        send(r_y, r_yin.at[d], ry_s.at[d], ry_r.at[d], at_y(d))

    for d in range(1, NX):
        arrive(g_xin.at[d], gx_s.at[d], gx_r.at[d])
        gram = gram + g_xin[d]
    rows_c = pl.ds(pl.multiple_of(RANK // 2 * c, RANK // 2), RANK // 2)
    rows_o = pl.ds(pl.multiple_of(RANK // 2 * o, RANK // 2), RANK // 2)
    g_all[rows_c, :] = gram
    send(g_all.at[rows_c], g_all.at[rows_c], gc_s.at[0], gc_r.at[0], sibling)
    arrive(g_all.at[rows_o], gc_s.at[0], gc_r.at[0])
    inverse = invert_steps(g_all[...], 10)

    term = r_y[...]
    for d in range(1, NY):
        arrive(r_yin.at[d], ry_s.at[d], ry_r.at[d])
        term = term + r_yin[d]
    r_all[:, rank_of(0), :] = term
    for d in AROUND_4:
        send(r_all.at[:, rank_of(0)], r_all.at[:, rank_of(0)], ra_s.at[d], ra_r.at[d], at_x(d))
    inverse = invert_steps(inverse, 6)
    ortho_out[...] = dot(l_all[...], inverse, HIGHEST) * (1.0 / 16.0)
    for copy in sends:
        copy.wait_send()

    @pl.when(mine)
    def _():
        for copy in y_copies():
            copy.wait_send()

    for d in range(1, NX):
        arrive(r_all.at[:, rank_of(NX - d)], ra_s.at[d], ra_r.at[d])


def update(ortho, right, params, momentum, new_params, new_momentum):
    for h in range(2):
        cols = slice(h * RANK, (h + 1) * RANK)
        grad = dot(ortho[...], right[h], HIGHEST)
        updated = outer_decay * momentum[:, cols] + grad
        new_momentum[:, cols] = updated
        new_params[:, cols] = params[:, cols] - outer_rate * (grad + outer_decay * updated)


def body(island_deltas, start_basis, outer_params, momentum):
    dma = pltpu.SemaphoreType.DMA
    vmem = pltpu.VMEM
    pair = lambda *shape: [dma(shape), dma(shape)]
    scratch = [
        vmem((SHARD, RANK), BF16),
        vmem((ROWS, NZ * BLOCK), BF16),
        vmem((ROWS, NZ * BLOCK), BF16),
        vmem((NZ * BLOCK, RANK), BF16),
        vmem((ROWS, RANK), F32),
        vmem((HALF, RANK), F32),
        vmem((HALF, RANK), F32),
        vmem((NZ, PIECE, RANK), F32),
        vmem((ROWS, RANK), F32),
        vmem((NZ, RANK, RANK), F32),
        vmem((NZ, RANK, RANK), BF16),
        vmem((NX, NZ, SLICE, RANK), BF16),
        vmem((NZ, SLICE, RANK), F32),
        vmem((NZ, SLICE, RANK), F32),
        vmem((RANK, RANK), F32),
        vmem((NZ, RANK, RANK), BF16),
        vmem((NZ, RANK, RANK), BF16),
        vmem((RANK, RANK), F32),
        vmem((NX, SLICE, RANK), F32),
        vmem((2, SLICE, RANK), F32),
        vmem((NY, 2, SLICE, RANK), F32),
        vmem((RANK // 2, RANK), F32),
        vmem((NY, RANK // 2, RANK), F32),
        vmem((RANK // 2, RANK), F32),
        vmem((NX, RANK // 2, RANK), F32),
        vmem((RANK, RANK), F32),
        dma((NZ + 1,)),
        *pair(NZ),
        dma((NY,)),
        dma((4,)),
        *pair(NX, 4),
        *pair(1),
        *pair(NZ),
        *pair(NZ),
        *pair(NZ),
        *pair(NX, 2),
        *pair(NZ),
        *pair(NZ),
        *pair(NX),
        *pair(NY),
        *pair(NX),
        *pair(NY),
        *pair(NX),
        *pair(1),
    ]
    in_vmem = pl.BlockSpec(memory_space=pltpu.VMEM)
    ortho, right = pl.pallas_call(
        kernel,
        name="factors",
        out_shape=(jax.ShapeDtypeStruct((ROWS, RANK), F32), jax.ShapeDtypeStruct((2, RANK, RANK), F32)),
        in_specs=[pl.BlockSpec(memory_space=pl.ANY)] * 2,
        out_specs=(in_vmem, in_vmem),
        scratch_shapes=scratch,
        compiler_params=pltpu.CompilerParams(
            collective_id=0, has_side_effects=True, vmem_limit_bytes=24 * 1024 * 1024
        ),
    )(
        pltpu.with_memory_space_constraint(island_deltas, pltpu.HBM),
        pltpu.with_memory_space_constraint(start_basis, pltpu.HBM),
    )
    state = jax.ShapeDtypeStruct(outer_params.shape, F32)
    return tuple(
        pl.pallas_call(
            update,
            name="update",
            out_shape=(state, state),
            in_specs=[in_vmem] * 4,
            out_specs=(in_vmem, in_vmem),
            compiler_params=pltpu.CompilerParams(vmem_limit_bytes=8 * 1024 * 1024),
        )(ortho, right, outer_params, momentum)
    )


def solution(mesh):
    placed = (
        P("island", "shard", None),
        P("shard", None),
        P("shard", "island"),
        P("shard", "island"),
    )
    return jax.shard_map(
        body,
        mesh=mesh,
        in_specs=placed,
        out_specs=(P("shard", "island"), P("shard", "island")),
        check_vma=False,
    )
```

```python
import functools

import jax
import jax.numpy as jnp
from jax import lax
from jax.experimental import pallas as pl
from jax.experimental.pallas import tpu as pltpu
from jax.sharding import PartitionSpec as P

outer_rate = 0.7
outer_decay = 0.9

MESH = pl.DeviceIdType.MESH
F32 = jnp.float32
BF16 = jnp.bfloat16
HIGHEST = lax.Precision.HIGHEST

NX, NY, NZ = 4, 8, 8
ROWS = 384
RANK = 128
HALF = ROWS // 2
PIECE = HALF // NZ
BLOCK = 256
SHARD = 128
SLICE = RANK // NX


AROUND_8 = (4, 3, 5, 2, 6, 1, 7)
AROUND_4 = (2, 1, 3)


def dot(a, b, precision=None):
    return jnp.dot(a, b, preferred_element_type=F32, precision=precision)


def invert_steps(a, steps):
    lane = lax.broadcasted_iota(jnp.int32, (8, RANK), 1)
    row = lax.broadcasted_iota(jnp.int32, (8, RANK), 0)

    def step(_, a):
        panel = a[0:8, :]
        columns = [jnp.broadcast_to(panel[:, j : j + 1], (8, RANK)) for j in range(8)]
        panel = jnp.where(lane < 8, (lane == row).astype(F32), panel)
        for j in range(8):
            here = row == j
            pivot = 1.0 / jnp.broadcast_to(columns[j][j : j + 1, :], (8, RANK))

            def reduced(values, j=j, here=here, pivot=pivot):
                scaled = jnp.broadcast_to(values[j : j + 1, :], (8, RANK)) * pivot
                return jnp.where(here, scaled, values - columns[j] * scaled)

            panel = reduced(panel)
            for m in range(j + 1, 8):
                columns[m] = reduced(columns[m])
        rest = a[8:, :]
        kept = jnp.where(lax.broadcasted_iota(jnp.int32, rest.shape, 1) < 8, 0.0, rest)
        for j in range(8):
            kept = kept - jnp.broadcast_to(rest[:, j : j + 1], rest.shape) * jnp.broadcast_to(
                panel[j : j + 1, :], rest.shape
            )
        return pltpu.roll(jnp.concatenate([kept, panel], axis=0), RANK - 8, 1)

    return lax.fori_loop(0, steps, step, a)


def kernel(
    deltas, basis, ortho_out, r_all,
    basis_v, d_own, d_sib, s_all, l_part, l_sib, l_half, l_in, l_all,
    a_f32, a_b16, a_x, a_z, a_zin, b_f32, b_b16, b_zin, b_x, b_xin, r_y, r_yin,
    g_own, g_yin, g_x, g_xin, g_all,
    load_sem, basis_sem,
    ds_s, ds_r, sy_s, sy_r, sx_s, sx_r, lc_s, lc_r, lz_s, lz_r, la_s, la_r, lf_s, lf_r,
    ax_s, ax_r, az_s, az_r, bz_s, bz_r, bx_s, bx_r, ry_s, ry_r, ra_s, ra_r, gy_s, gy_r, gx_s, gx_r, gc_s, gc_r,
):
    island = lax.axis_index("island")
    shard = lax.axis_index("shard")
    z, c = island // 2, lax.rem(island, 2)
    x, y = shard // NY, lax.rem(shard, NY)
    o = 1 - c

    def at_x(d):
        return (island, lax.rem(x + d, NX) * NY + y)

    def at_y(d):
        return (island, x * NY + lax.rem(y + d, NY))

    def at_z(d):
        return (lax.rem(z + d, NZ) * 2 + c, shard)

    sibling = (z * 2 + o, shard)
    def send(src, dst, s, r, device):
        pltpu.make_async_remote_copy(
            src_ref=src, dst_ref=dst, send_sem=s, recv_sem=r, device_id=device, device_id_type=MESH
        ).start()

    def whole_copy(whole, sem):
        return pltpu.make_async_remote_copy(
            src_ref=whole, dst_ref=whole, send_sem=sem, recv_sem=sem, device_id=sibling, device_id_type=MESH
        )

    def arrive(whole, r):
        whole_copy(whole, r).wait_recv()

    def sent(whole, s):
        whole_copy(whole, s).wait_send()

    barrier = pltpu.get_barrier_semaphore()
    partners = [at_y(d) for d in range(1, NY)] + [at_z(d) for d in range(1, NZ)] + [at_x(d) for d in range(1, NX)]
    for device in partners + [sibling]:
        pl.semaphore_signal(barrier, inc=1, device_id=device, device_id_type=MESH)

    basis_load = pltpu.make_async_copy(basis, basis_v, basis_sem)
    basis_load.start()
    for b in range(NZ):
        cols = pl.ds(pl.multiple_of((2 * b + c) * BLOCK, BLOCK), BLOCK)
        pltpu.make_async_copy(deltas.at[0, :, cols], d_own.at[:, pl.ds(b * BLOCK, BLOCK)], load_sem).start()

    basis_load.wait()
    pl.semaphore_wait(barrier, len(partners) + 1)

    mine = lax.rem(y // 2, 2) == c
    own_slot = 4 * x + 2 * (y // 4) + lax.rem(y, 2)

    def slot(index):
        return s_all.at[pl.ds(pl.multiple_of(index * SHARD, SHARD), SHARD)]

    @pl.when(mine)
    def _():
        for d in AROUND_8:
            send(basis_v, slot(own_slot), sy_s, sy_r.at[own_slot - 4 * x], at_y(d))
        slot(own_slot)[...] = basis_v[...]

    for b in range(NZ):
        cols = pl.ds(pl.multiple_of((2 * b + o) * BLOCK, BLOCK), BLOCK)
        send(deltas.at[0, :, cols], d_sib.at[:, pl.ds(b * BLOCK, BLOCK)], ds_s, ds_r, sibling)

    turn = 1 - 2 * lax.rem(y, 2)
    order = [jnp.where(mine, a, b) * turn for a, b in ((0, -1), (1, 2), (-3, -2), (4, 3))]
    for n, offset in enumerate(order):
        source = lax.rem(y + offset + NY, NY)
        k = lax.rem(source, 2) + 2 * (source // 4)
        if n == 0:

            @pl.when(jnp.logical_not(mine))
            def _():
                arrive(slot(4 * x + k), sy_r.at[k])
        else:
            arrive(slot(4 * x + k), sy_r.at[k])
        for d in AROUND_4:
            send(slot(4 * x + k), slot(4 * x + k), sx_s, sx_r.at[d - 1], at_x(d))

    pltpu.make_async_copy(d_own, d_own, load_sem).wait()
    arrive(d_sib, ds_r)

    def quarter(d):
        return pl.ds(pl.multiple_of(4 * SHARD * lax.rem(x + NX - d, NX), 4 * SHARD), 4 * SHARD)

    def left_term(d):
        cols = quarter(d)
        return dot(d_own[:, cols], s_all[cols, :]) + dot(d_sib[:, cols], s_all[cols, :])

    l_part[...] = left_term(0)
    for d in (1, 3, 2):
        arrive(s_all.at[quarter(d)], sx_r.at[d - 1])
        l_part[...] += left_term(d)
    send(l_part.at[pl.ds(pl.multiple_of(HALF * o, HALF), HALF)], l_sib, lc_s, lc_r, sibling)
    arrive(l_sib, lc_r)
    l_half[...] = l_part[pl.ds(pl.multiple_of(HALF * c, HALF), HALF), :] + l_sib[...]
    for d in AROUND_8:
        rows = pl.ds(pl.multiple_of(PIECE * lax.rem(z + d, NZ), 8), PIECE)
        send(l_half.at[rows], l_in.at[d], lz_s, lz_r, at_z(d))
    total = l_half[pl.ds(pl.multiple_of(PIECE * z, 8), PIECE), :]
    arrive(l_in.at[pl.ds(1, NZ - 1)], lz_r)
    for d in range(1, NZ):
        total = total + l_in[d]

    own_half = l_all.at[pl.ds(pl.multiple_of(HALF * c, HALF), HALF)]
    piece = l_all.at[pl.ds(pl.multiple_of(HALF * c + PIECE * z, 8), PIECE)]
    piece[...] = total
    others = l_half.at[pl.ds(0, HALF - PIECE)]
    for d in AROUND_8:
        send(piece, piece, la_s, la_r, at_z(d))
    arrive(others, la_r)
    send(own_half, own_half, lf_s, lf_r, sibling)
    arrive(l_half, lf_r)

    left = l_all[...]
    left_t = left.T
    high = left_t.astype(BF16)
    low = (left_t - high.astype(F32)).astype(BF16)
    both = jnp.concatenate([high, low], axis=0)

    def rank_of(d):
        return pl.ds(pl.multiple_of(SLICE * lax.rem(x + d, NX), SLICE), SLICE)

    for n, away in enumerate((*AROUND_8, 0)):
        cols = pl.ds(pl.multiple_of(BLOCK * lax.rem(z + away, NZ), BLOCK), BLOCK)
        term = dot(both, d_own[:, cols]) + dot(both, d_sib[:, cols])
        term = term[:RANK] + term[RANK:]
        a_f32[n] = term[:, :RANK]
        a_b16[n] = term[:, :RANK].astype(BF16)
        if away:
            b_b16[n] = term[:, RANK:].astype(BF16)
            send(b_b16.at[n], b_zin.at[n], bz_s, bz_r, at_z(away))
        else:
            b_f32[...] = term[:, RANK:]
        if n % 4 == 3:
            h = n // 4
            part = pl.ds(4 * h, 4)
            for d in AROUND_4:
                send(a_b16.at[part, rank_of(d)], a_x.at[d, part], ax_s, ax_r.at[h], at_x(d))

    g_part = dot(left_t, left, HIGHEST)
    g_own[...] = jnp.where(c == 0, g_part[: RANK // 2], g_part[RANK // 2 :])
    for d in AROUND_8:
        send(g_own, g_yin.at[d], gy_s, gy_r, at_y(d))

    for h in range(2):
        arrive(a_x.at[pl.ds(1, NX - 1), pl.ds(4 * h, 4)], ax_r.at[h])
        for n in range(4 * h, 4 * h + 4):
            term = a_f32[n, rank_of(0), :]
            for d in range(1, NX):
                term = term + a_x[d, n].astype(F32)
            a_z[n] = term
            if n < NZ - 1:
                send(a_z.at[n], a_zin.at[n], az_s, az_r, at_z(AROUND_8[n]))

    b_sum = b_f32[...]
    arrive(b_zin.at[pl.ds(0, NZ - 1)], bz_r)
    for n in range(NZ - 1):
        b_sum = b_sum + b_zin[n].astype(F32)
    b_x[...] = b_sum
    for d in AROUND_4:
        send(b_x.at[rank_of(d)], b_xin.at[d], bx_s, bx_r, at_x(d))

    gram = g_own[...]
    arrive(g_yin.at[pl.ds(1, NY - 1)], gy_r)
    for d in range(1, NY):
        gram = gram + g_yin[d]
    g_x[...] = gram
    for d in AROUND_4:
        send(g_x, g_xin.at[d], gx_s, gx_r, at_x(d))

    a_sum = a_z[NZ - 1]
    arrive(a_zin.at[pl.ds(0, NZ - 1)], az_r)
    for n in range(NZ - 1):
        a_sum = a_sum + a_zin[n]
    b_sum = b_x[rank_of(0), :]
    arrive(b_xin.at[pl.ds(1, NX - 1)], bx_r)
    for d in range(1, NX):
        b_sum = b_sum + b_xin[d]
    r_y[0] = a_sum
    r_y[1] = b_sum
    for d in AROUND_8:
        send(r_y, r_yin.at[d], ry_s, ry_r, at_y(d))

    arrive(g_xin.at[pl.ds(1, NX - 1)], gx_r)
    for d in range(1, NX):
        gram = gram + g_xin[d]
    rows_c = pl.ds(pl.multiple_of(RANK // 2 * c, RANK // 2), RANK // 2)
    rows_o = pl.ds(pl.multiple_of(RANK // 2 * o, RANK // 2), RANK // 2)
    g_all[rows_c, :] = gram
    send(g_all.at[rows_c], g_all.at[rows_c], gc_s, gc_r, sibling)
    arrive(g_all.at[rows_o], gc_r)
    inverse = invert_steps(g_all[...], 10)

    term = r_y[...]
    arrive(r_yin.at[pl.ds(1, NY - 1)], ry_r)
    for d in range(1, NY):
        term = term + r_yin[d]
    r_all[:, rank_of(0), :] = term
    for d in AROUND_4:
        send(r_all.at[:, rank_of(0)], r_all.at[:, rank_of(0)], ra_s, ra_r, at_x(d))
    inverse = invert_steps(inverse, 6)
    ortho_out[...] = dot(l_all[...], inverse, HIGHEST) * (1.0 / 16.0)

    @pl.when(mine)
    def _():
        sent(s_all.at[pl.ds(0, (NY - 1) * SHARD)], sy_s)

    sent(d_sib, ds_s)
    sent(s_all.at[pl.ds(0, 4 * (NX - 1) * SHARD)], sx_s)
    sent(l_half, lc_s)
    sent(others, lz_s)
    sent(others, la_s)
    sent(l_half, lf_s)
    sent(a_b16.at[pl.ds(0, 2 * (NX - 1))], ax_s)
    sent(a_z.at[pl.ds(0, NZ - 1)], az_s)
    sent(b_b16.at[pl.ds(0, NZ - 1)], bz_s)
    sent(b_x.at[pl.ds(0, (NX - 1) * SLICE)], bx_s)
    sent(r_yin.at[pl.ds(0, NY - 1)], ry_s)
    sent(g_yin.at[pl.ds(0, NY - 1)], gy_s)
    sent(g_xin.at[pl.ds(0, NX - 1)], gx_s)
    sent(g_x, gc_s)
    arrive(r_yin.at[pl.ds(0, NX - 1)], ra_r)
    sent(r_yin.at[pl.ds(0, NX - 1)], ra_s)


def update(ortho, right, params, momentum, new_params, new_momentum):
    for h in range(2):
        cols = slice(h * RANK, (h + 1) * RANK)
        grad = dot(ortho[...], right[h], HIGHEST)
        updated = outer_decay * momentum[:, cols] + grad
        new_momentum[:, cols] = updated
        new_params[:, cols] = params[:, cols] - outer_rate * (grad + outer_decay * updated)


def body(island_deltas, start_basis, outer_params, momentum):
    dma = pltpu.SemaphoreType.DMA
    vmem = pltpu.VMEM
    scratch = [
        vmem((SHARD, RANK), BF16),
        vmem((ROWS, NZ * BLOCK), BF16),
        vmem((ROWS, NZ * BLOCK), BF16),
        vmem((NZ * BLOCK, RANK), BF16),
        vmem((ROWS, RANK), F32),
        vmem((HALF, RANK), F32),
        vmem((HALF, RANK), F32),
        vmem((NZ, PIECE, RANK), F32),
        vmem((ROWS, RANK), F32),
        vmem((NZ, RANK, RANK), F32),
        vmem((NZ, RANK, RANK), BF16),
        vmem((NX, NZ, SLICE, RANK), BF16),
        vmem((NZ, SLICE, RANK), F32),
        vmem((NZ, SLICE, RANK), F32),
        vmem((RANK, RANK), F32),
        vmem((NZ, RANK, RANK), BF16),
        vmem((NZ, RANK, RANK), BF16),
        vmem((RANK, RANK), F32),
        vmem((NX, SLICE, RANK), F32),
        vmem((2, SLICE, RANK), F32),
        vmem((NY, 2, SLICE, RANK), F32),
        vmem((RANK // 2, RANK), F32),
        vmem((NY, RANK // 2, RANK), F32),
        vmem((RANK // 2, RANK), F32),
        vmem((NX, RANK // 2, RANK), F32),
        vmem((RANK, RANK), F32),
        *[dma(())] * 2,
        *[dma(())] * 2,
        dma(()),
        dma((4,)),
        dma(()),
        dma((NX - 1,)),
        *[dma(())] * 8,
        dma(()),
        dma((2,)),
        *[dma(())] * 16,
    ]
    in_vmem = pl.BlockSpec(memory_space=pltpu.VMEM)
    ortho, right = pl.pallas_call(
        kernel,
        name="factors",
        out_shape=(jax.ShapeDtypeStruct((ROWS, RANK), F32), jax.ShapeDtypeStruct((2, RANK, RANK), F32)),
        in_specs=[pl.BlockSpec(memory_space=pl.ANY)] * 2,
        out_specs=(in_vmem, in_vmem),
        scratch_shapes=scratch,
        compiler_params=pltpu.CompilerParams(
            collective_id=0, has_side_effects=True, vmem_limit_bytes=24 * 1024 * 1024
        ),
    )(
        pltpu.with_memory_space_constraint(island_deltas, pltpu.HBM),
        pltpu.with_memory_space_constraint(start_basis, pltpu.HBM),
    )
    state = jax.ShapeDtypeStruct(outer_params.shape, F32)
    return tuple(
        pl.pallas_call(
            update,
            name="update",
            out_shape=(state, state),
            in_specs=[in_vmem] * 4,
            out_specs=(in_vmem, in_vmem),
            compiler_params=pltpu.CompilerParams(vmem_limit_bytes=8 * 1024 * 1024),
        )(ortho, right, outer_params, momentum)
    )


def solution(mesh):
    placed = (
        P("island", "shard", None),
        P("shard", None),
        P("shard", "island"),
        P("shard", "island"),
    )
    return jax.shard_map(
        body,
        mesh=mesh,
        in_specs=placed,
        out_specs=(P("shard", "island"), P("shard", "island")),
        check_vma=False,
    )
```

```python
import functools

import jax
import jax.numpy as jnp
from jax import lax
from jax.experimental import pallas as pl
from jax.experimental.pallas import tpu as pltpu
from jax.sharding import PartitionSpec as P

outer_rate = 0.7
outer_decay = 0.9

MESH = pl.DeviceIdType.MESH
F32 = jnp.float32
BF16 = jnp.bfloat16
HIGHEST = lax.Precision.HIGHEST

NX, NY, NZ = 4, 8, 8
ROWS = 384
RANK = 128
HALF = ROWS // 2
STRIP = ROWS // 3
PIECE = HALF // NZ
BLOCK = 256
SHARD = 128
SLICE = RANK // NX
PART = SLICE // 2


AROUND_8 = (4, 3, 5, 2, 6, 1, 7)
AROUND_4 = (2, 1, 3)


def dot(a, b, precision=None):
    return jnp.dot(a, b, preferred_element_type=F32, precision=precision)


def invert_steps(a, steps):
    lane = lax.broadcasted_iota(jnp.int32, (8, RANK), 1)
    row = lax.broadcasted_iota(jnp.int32, (8, RANK), 0)

    def step(_, a):
        panel = a[0:8, :]
        columns = [jnp.broadcast_to(panel[:, j : j + 1], (8, RANK)) for j in range(8)]
        panel = jnp.where(lane < 8, (lane == row).astype(F32), panel)
        for j in range(8):
            here = row == j
            pivot = 1.0 / jnp.broadcast_to(columns[j][j : j + 1, :], (8, RANK))

            def reduced(values, j=j, here=here, pivot=pivot):
                scaled = jnp.broadcast_to(values[j : j + 1, :], (8, RANK)) * pivot
                return jnp.where(here, scaled, values - columns[j] * scaled)

            panel = reduced(panel)
            for m in range(j + 1, 8):
                columns[m] = reduced(columns[m])
        rest = a[8:, :]
        kept = jnp.where(lax.broadcasted_iota(jnp.int32, rest.shape, 1) < 8, 0.0, rest)
        for j in range(8):
            kept = kept - jnp.broadcast_to(rest[:, j : j + 1], rest.shape) * jnp.broadcast_to(
                panel[j : j + 1, :], rest.shape
            )
        return pltpu.roll(jnp.concatenate([kept, panel], axis=0), RANK - 8, 1)

    return lax.fori_loop(0, steps, step, a)


def kernel(
    deltas, basis, ortho_out, r_all,
    basis_v, d_own, d_sib, s_all, l_part, l_sib, l_half, l_in, l_all,
    a_f32, a_b16, a_x, a_z, a_zin, b_f32, b_b16, b_zin, b_x, b_xin, r_y, r_yin,
    g_own, g_yin, g_xin, g_sum, g_all,
    load_sem, basis_sem,
    ds_s, ds_r, sy_s, sy_r, sx_s, sx_r, lc_s, lc_r, lz_s, lz_r, la_s, la_r, lf_s, lf_r,
    ax_s, ax_r, az_s, az_r, bz_s, bz_r, bx_s, bx_r, ry_s, ry_r, ra_s, ra_r, gy_s, gy_r, gx_s, gx_r, gc_s, gc_r,
):
    island = lax.axis_index("island")
    shard = lax.axis_index("shard")
    z, c = island // 2, lax.rem(island, 2)
    x, y = shard // NY, lax.rem(shard, NY)
    o = 1 - c

    def at_x(d):
        return (island, lax.rem(x + d, NX) * NY + y)

    def at_y(d):
        return (island, x * NY + lax.rem(y + d, NY))

    def at_z(d):
        return (lax.rem(z + d, NZ) * 2 + c, shard)

    sibling = (z * 2 + o, shard)
    def send(src, dst, s, r, device):
        pltpu.make_async_remote_copy(
            src_ref=src, dst_ref=dst, send_sem=s, recv_sem=r, device_id=device, device_id_type=MESH
        ).start()

    def whole_copy(whole, sem):
        return pltpu.make_async_remote_copy(
            src_ref=whole, dst_ref=whole, send_sem=sem, recv_sem=sem, device_id=sibling, device_id_type=MESH
        )

    def arrive(whole, r):
        whole_copy(whole, r).wait_recv()

    def sent(whole, s):
        whole_copy(whole, s).wait_send()

    barrier = pltpu.get_barrier_semaphore()
    partners = [at_y(d) for d in range(1, NY)] + [at_z(d) for d in range(1, NZ)] + [at_x(d) for d in range(1, NX)]
    for device in partners + [sibling]:
        pl.semaphore_signal(barrier, inc=1, device_id=device, device_id_type=MESH)

    basis_load = pltpu.make_async_copy(basis, basis_v, basis_sem)
    basis_load.start()
    for b in range(NZ):
        cols = pl.ds(pl.multiple_of((2 * b + c) * BLOCK, BLOCK), BLOCK)
        pltpu.make_async_copy(deltas.at[0, :, cols], d_own.at[:, pl.ds(b * BLOCK, BLOCK)], load_sem).start()

    basis_load.wait()
    pl.semaphore_wait(barrier, len(partners) + 1)

    mine = lax.rem(y // 2, 2) == c
    own_slot = 4 * x + 2 * (y // 4) + lax.rem(y, 2)

    def slot(index):
        return s_all.at[pl.ds(pl.multiple_of(index * SHARD, SHARD), SHARD)]

    @pl.when(mine)
    def _():
        for d in (1, 7, 4, 2, 6, 3, 5):
            send(basis_v, slot(own_slot), sy_s, sy_r.at[own_slot - 4 * x], at_y(d))
        slot(own_slot)[...] = basis_v[...]

    for b in range(NZ):
        cols = pl.ds(pl.multiple_of((2 * b + o) * BLOCK, BLOCK), BLOCK)
        send(deltas.at[0, :, cols], d_sib.at[:, pl.ds(b * BLOCK, BLOCK)], ds_s, ds_r, sibling)

    turn = 1 - 2 * lax.rem(y, 2)
    order = [jnp.where(mine, a, b) * turn for a, b in ((0, -1), (1, 2), (-3, -2), (4, 3))]
    for n, offset in enumerate(order):
        source = lax.rem(y + offset + NY, NY)
        k = lax.rem(source, 2) + 2 * (source // 4)
        if n == 0:

            @pl.when(jnp.logical_not(mine))
            def _():
                arrive(slot(4 * x + k), sy_r.at[k])
        else:
            arrive(slot(4 * x + k), sy_r.at[k])
        for d in AROUND_4:
            send(slot(4 * x + k), slot(4 * x + k), sx_s, sx_r.at[d - 1], at_x(d))

    pltpu.make_async_copy(d_own, d_own, load_sem).wait()
    arrive(d_sib, ds_r)

    def quarter(d):
        return pl.ds(pl.multiple_of(4 * SHARD * lax.rem(x + NX - d, NX), 4 * SHARD), 4 * SHARD)

    def left_term(d):
        cols = quarter(d)
        return dot(d_own[:, cols], s_all[cols, :]) + dot(d_sib[:, cols], s_all[cols, :])

    l_part[...] = left_term(0)
    for d in (1, 3, 2):
        arrive(s_all.at[quarter(d)], sx_r.at[d - 1])
        l_part[...] += left_term(d)
    send(l_part.at[pl.ds(pl.multiple_of(HALF * o, HALF), HALF)], l_sib, lc_s, lc_r, sibling)
    arrive(l_sib, lc_r)
    l_half[...] = l_part[pl.ds(pl.multiple_of(HALF * c, HALF), HALF), :] + l_sib[...]
    for d in AROUND_8:
        rows = pl.ds(pl.multiple_of(PIECE * lax.rem(z + d, NZ), 8), PIECE)
        send(l_half.at[rows], l_in.at[d], lz_s, lz_r, at_z(d))
    total = l_half[pl.ds(pl.multiple_of(PIECE * z, 8), PIECE), :]
    arrive(l_in.at[pl.ds(1, NZ - 1)], lz_r)
    for d in range(1, NZ):
        total = total + l_in[d]

    own_half = l_all.at[pl.ds(pl.multiple_of(HALF * c, HALF), HALF)]
    piece = l_all.at[pl.ds(pl.multiple_of(HALF * c + PIECE * z, 8), PIECE)]
    piece[...] = total
    others = l_half.at[pl.ds(0, HALF - PIECE)]
    for d in AROUND_8:
        send(piece, piece, la_s, la_r, at_z(d))
    arrive(others, la_r)
    send(own_half, own_half, lf_s, lf_r, sibling)
    arrive(l_half, lf_r)

    left = l_all[...]
    left_t = left.T

    g_part = dot(left_t, left, HIGHEST)
    g_own[...] = jnp.where(c == 0, g_part[: RANK // 2], g_part[RANK // 2 :])
    first, second = pl.ds(0, RANK // 4), pl.ds(RANK // 4, RANK // 4)
    for d in AROUND_8:
        send(g_own.at[first], g_yin.at[0, d], gy_s, gy_r.at[0], at_y(d))
    for d in AROUND_4:
        send(g_own.at[second], g_xin.at[1, d], gx_s, gx_r.at[1], at_x(d))

    high = left_t.astype(BF16)
    low = (left_t - high.astype(F32)).astype(BF16)
    both = jnp.concatenate([high, low], axis=0)

    def rank_of(d):
        return pl.ds(pl.multiple_of(SLICE * lax.rem(x + d, NX), SLICE), SLICE)

    def send_b(n, q):
        send(b_b16.at[q, n], b_zin.at[q, n], bz_s, bz_r.at[q], at_z(AROUND_8[n]))

    for n, away in enumerate((*AROUND_8, 0)):
        cols = pl.ds(pl.multiple_of(BLOCK * lax.rem(z + away, NZ), BLOCK), BLOCK)
        term = dot(both, d_own[:, cols]) + dot(both, d_sib[:, cols])
        term = term[:RANK] + term[RANK:]
        a_f32[n] = term[:, :RANK]
        a_b16[n] = term[:, :RANK].astype(BF16)
        for q in range(2):
            for i in range(NX):
                rows = slice(SLICE * i + PART * q, SLICE * i + PART * (q + 1))
                if away:
                    b_b16[q, n, i] = term[rows, RANK:].astype(BF16)
                else:
                    b_f32[q, i] = term[rows, RANK:]
        if away:
            send_b(n, 0)
        if n % 4 == 3:
            h = n // 4
            part = pl.ds(4 * h, 4)
            for d in AROUND_4:
                send(a_b16.at[part, rank_of(d)], a_x.at[d, part], ax_s, ax_r.at[h], at_x(d))
    for n in range(NZ - 1):
        send_b(n, 1)

    others_x, others_y, others_z = pl.ds(1, NX - 1), pl.ds(1, NY - 1), pl.ds(0, NZ - 1)
    arrive(g_xin.at[1, others_x], gx_r.at[1])
    g_second = g_own[second, :]
    for d in range(1, NX):
        g_second = g_second + g_xin[1, d]
    g_sum[1] = g_second
    for d in AROUND_8:
        send(g_sum.at[1], g_yin.at[1, d], gy_s, gy_r.at[1], at_y(d))

    def send_a(n, q):
        send(a_z.at[q, n], a_zin.at[q, n], az_s, az_r.at[q], at_z(AROUND_8[n]))

    for h in range(2):
        arrive(a_x.at[others_x, pl.ds(4 * h, 4)], ax_r.at[h])
        for n in range(4 * h, 4 * h + 4):
            term = a_f32[n, rank_of(0), :]
            for d in range(1, NX):
                term = term + a_x[d, n].astype(F32)
            a_z[0, n] = term[:PART]
            a_z[1, n] = term[PART:]
            if n < NZ - 1:
                send_a(n, 0)
    for n in range(NZ - 1):
        send_a(n, 1)

    def sum_b(q):
        arrive(b_zin.at[q, others_z], bz_r.at[q])
        total = b_f32[q]
        for n in range(NZ - 1):
            total = total + b_zin[q, n].astype(F32)
        b_x[q] = total
        for d in AROUND_4:
            send(b_x.at[q, lax.rem(x + d, NX)], b_xin.at[q, d], bx_s, bx_r.at[q], at_x(d))

    def send_y(u):
        for d in AROUND_8:
            send(r_y.at[u], r_yin.at[u, d], ry_s, ry_r.at[u], at_y(d))

    def end_a(q):
        arrive(a_zin.at[q, others_z], az_r.at[q])
        total = a_z[q, NZ - 1]
        for n in range(NZ - 1):
            total = total + a_zin[q, n]
        r_y[q] = total
        send_y(q)

    def end_b(q):
        arrive(b_xin.at[q, others_x], bx_r.at[q])
        total = b_x[q, x]
        for d in range(1, NX):
            total = total + b_xin[q, d]
        r_y[2 + q] = total
        send_y(2 + q)

    sum_b(0)
    arrive(g_yin.at[0, others_y], gy_r.at[0])
    g_first = g_own[first, :]
    for d in range(1, NY):
        g_first = g_first + g_yin[0, d]
    g_sum[0] = g_first
    for d in AROUND_4:
        send(g_sum.at[0], g_xin.at[0, d], gx_s, gx_r.at[0], at_x(d))
    sum_b(1)
    end_b(0)
    arrive(g_xin.at[0, others_x], gx_r.at[0])
    for d in range(1, NX):
        g_first = g_first + g_xin[0, d]
    arrive(g_yin.at[1, others_y], gy_r.at[1])
    for d in range(1, NY):
        g_second = g_second + g_yin[1, d]
    rows_c = pl.ds(pl.multiple_of(RANK // 2 * c, RANK // 2), RANK // 2)
    rows_o = pl.ds(pl.multiple_of(RANK // 2 * o, RANK // 2), RANK // 2)
    g_all[rows_c, :] = jnp.concatenate([g_first, g_second], axis=0)
    send(g_all.at[rows_c], g_all.at[rows_c], gc_s, gc_r, sibling)
    end_a(0)
    end_a(1)
    end_b(1)

    arrive(g_all.at[rows_o], gc_r)
    inverse = invert_steps(g_all[...], 16)

    for u in (2, 0, 1, 3):
        arrive(r_yin.at[u, others_y], ry_r.at[u])
        total = r_y[u]
        for d in range(1, NY):
            total = total + r_yin[u, d]
        here = r_all.at[u // 2, pl.ds(pl.multiple_of(SLICE * x + PART * (u % 2), PART), PART)]
        here[...] = total
        for d in AROUND_4:
            send(here, here, ra_s, ra_r, at_x(d))
    ortho_out[...] = dot(l_all[...], inverse, HIGHEST) * (1.0 / 16.0)

    @pl.when(mine)
    def _():
        sent(s_all.at[pl.ds(0, (NY - 1) * SHARD)], sy_s)

    sent(d_sib, ds_s)
    sent(s_all.at[pl.ds(0, 4 * (NX - 1) * SHARD)], sx_s)
    sent(l_half, lc_s)
    sent(others, lz_s)
    sent(others, la_s)
    sent(l_half, lf_s)
    sent(a_b16.at[pl.ds(0, 2 * (NX - 1))], ax_s)
    sent(a_z.at[:, others_z], az_s)
    sent(b_b16.at[:, others_z], bz_s)
    sent(b_x.at[:, others_x], bx_s)
    sent(r_yin.at[:, others_y], ry_s)
    sent(g_yin.at[:, others_y], gy_s)
    sent(g_xin.at[:, others_x], gx_s)
    sent(g_own, gc_s)
    right_others = r_yin.at[:, others_x]
    arrive(right_others, ra_r)
    sent(right_others, ra_s)


def update(ortho, right, params, momentum, new_params, new_momentum, p_v, m_v, sem):
    stores = []
    for n in range(ROWS // STRIP):
        rows = slice(n * STRIP, (n + 1) * STRIP)
        for h in range(2):
            cols = slice(h * RANK, (h + 1) * RANK)
            grad = dot(ortho[rows, :], right[h], HIGHEST)
            updated = outer_decay * momentum[rows, cols] + grad
            m_v[rows, cols] = updated
            p_v[rows, cols] = params[rows, cols] - outer_rate * (grad + outer_decay * updated)
        for k, (src, dst) in enumerate(((m_v, new_momentum), (p_v, new_params))):
            copy = pltpu.make_async_copy(src.at[rows], dst.at[rows], sem.at[n, k])
            copy.start()
            stores.append(copy)
    for copy in stores:
        copy.wait()


def body(island_deltas, start_basis, outer_params, momentum):
    dma = pltpu.SemaphoreType.DMA
    vmem = pltpu.VMEM
    scratch = [
        vmem((SHARD, RANK), BF16),
        vmem((ROWS, NZ * BLOCK), BF16),
        vmem((ROWS, NZ * BLOCK), BF16),
        vmem((NZ * BLOCK, RANK), BF16),
        vmem((ROWS, RANK), F32),
        vmem((HALF, RANK), F32),
        vmem((HALF, RANK), F32),
        vmem((NZ, PIECE, RANK), F32),
        vmem((ROWS, RANK), F32),
        vmem((NZ, RANK, RANK), F32),
        vmem((NZ, RANK, RANK), BF16),
        vmem((NX, NZ, SLICE, RANK), BF16),
        vmem((2, NZ, PART, RANK), F32),
        vmem((2, NZ, PART, RANK), F32),
        vmem((2, NX, PART, RANK), F32),
        vmem((2, NZ, NX, PART, RANK), BF16),
        vmem((2, NZ, NX, PART, RANK), BF16),
        vmem((2, NX, PART, RANK), F32),
        vmem((2, NX, PART, RANK), F32),
        vmem((4, PART, RANK), F32),
        vmem((4, NY, PART, RANK), F32),
        vmem((RANK // 2, RANK), F32),
        vmem((2, NY, RANK // 4, RANK), F32),
        vmem((2, NX, RANK // 4, RANK), F32),
        vmem((2, RANK // 4, RANK), F32),
        vmem((RANK, RANK), F32),
        *[dma(())] * 2,
        *[dma(())] * 2,
        dma(()),
        dma((4,)),
        dma(()),
        dma((NX - 1,)),
        *[dma(())] * 8,
        dma(()),
        dma((2,)),
        *[dma(()), dma((2,))] * 3,
        *[dma(()), dma((4,))],
        *[dma(())] * 2,
        *[dma(()), dma((2,))] * 2,
        *[dma(())] * 2,
    ]
    in_vmem = pl.BlockSpec(memory_space=pltpu.VMEM)
    ortho, right = pl.pallas_call(
        kernel,
        name="factors",
        out_shape=(jax.ShapeDtypeStruct((ROWS, RANK), F32), jax.ShapeDtypeStruct((2, RANK, RANK), F32)),
        in_specs=[pl.BlockSpec(memory_space=pl.ANY)] * 2,
        out_specs=(in_vmem, in_vmem),
        scratch_shapes=scratch,
        compiler_params=pltpu.CompilerParams(
            collective_id=0, has_side_effects=True, vmem_limit_bytes=24 * 1024 * 1024
        ),
    )(
        pltpu.with_memory_space_constraint(island_deltas, pltpu.HBM),
        pltpu.with_memory_space_constraint(start_basis, pltpu.HBM),
    )
    state = jax.ShapeDtypeStruct(outer_params.shape, F32)
    return tuple(
        pl.pallas_call(
            update,
            name="update",
            out_shape=(state, state),
            in_specs=[in_vmem] * 4,
            out_specs=(pl.BlockSpec(memory_space=pl.ANY),) * 2,
            scratch_shapes=[vmem((ROWS, BLOCK), F32), vmem((ROWS, BLOCK), F32), dma((ROWS // STRIP, 2))],
            compiler_params=pltpu.CompilerParams(vmem_limit_bytes=8 * 1024 * 1024),
        )(ortho, right, outer_params, momentum)
    )


def solution(mesh):
    placed = (
        P("island", "shard", None),
        P("shard", None),
        P("shard", "island"),
        P("shard", "island"),
    )
    return jax.shard_map(
        body,
        mesh=mesh,
        in_specs=placed,
        out_specs=(P("shard", "island"), P("shard", "island")),
        check_vma=False,
    )
```

```python
import functools

import jax
import jax.numpy as jnp
from jax import lax
from jax.experimental import pallas as pl
from jax.experimental.pallas import tpu as pltpu
from jax.sharding import PartitionSpec as P

outer_rate = 0.7
outer_decay = 0.9

MESH = pl.DeviceIdType.MESH
F32 = jnp.float32
BF16 = jnp.bfloat16
HIGHEST = lax.Precision.HIGHEST

NX, NY, NZ = 4, 8, 8
ROWS = 384
RANK = 128
HALF = ROWS // 2
STRIP = ROWS // 3
PIECE = HALF // NZ
BLOCK = 256
SHARD = 128
SLICE = RANK // NX
PART = SLICE // 2


AROUND_8 = (4, 3, 5, 2, 6, 1, 7)
AROUND_4 = (1, 3, 2)


def dot(a, b, precision=None):
    return jnp.dot(a, b, preferred_element_type=F32, precision=precision)


def invert_steps(a, steps):
    lane = lax.broadcasted_iota(jnp.int32, (8, RANK), 1)
    row = lax.broadcasted_iota(jnp.int32, (8, RANK), 0)

    def step(_, a):
        panel = a[0:8, :]
        columns = [jnp.broadcast_to(panel[:, j : j + 1], (8, RANK)) for j in range(8)]
        panel = jnp.where(lane < 8, (lane == row).astype(F32), panel)
        for j in range(8):
            here = row == j
            pivot = 1.0 / jnp.broadcast_to(columns[j][j : j + 1, :], (8, RANK))

            def reduced(values, j=j, here=here, pivot=pivot):
                scaled = jnp.broadcast_to(values[j : j + 1, :], (8, RANK)) * pivot
                return jnp.where(here, scaled, values - columns[j] * scaled)

            panel = reduced(panel)
            for m in range(j + 1, 8):
                columns[m] = reduced(columns[m])
        rest = a[8:, :]
        kept = jnp.where(lax.broadcasted_iota(jnp.int32, rest.shape, 1) < 8, 0.0, rest)
        for j in range(8):
            kept = kept - jnp.broadcast_to(rest[:, j : j + 1], rest.shape) * jnp.broadcast_to(
                panel[j : j + 1, :], rest.shape
            )
        return pltpu.roll(jnp.concatenate([kept, panel], axis=0), RANK - 8, 1)

    return lax.fori_loop(0, steps, step, a)


def kernel(
    deltas, basis, ortho_out, r_all,
    basis_v, d_own, d_sib, s_all, l_part, l_sib, l_half, l_in, l_all,
    a_f32, a_b16, a_x, a_z, a_zin, b_f32, b_b16, b_zin, b_x, b_xin, r_y, r_yin,
    g_own, g_yin, g_xin, g_sum, g_all,
    load_sem, basis_sem,
    ds_s, ds_r, sy_s, sy_r, sx_s, sx_r, lc_s, lc_r, lz_s, lz_r, la_s, la_r, lf_s, lf_r,
    ax_s, ax_r, az_s, az_r, bz_s, bz_r, bx_s, bx_r, ry_s, ry_r, ra_s, ra_r, gy_s, gy_r, gx_s, gx_r, gc_s, gc_r,
):
    island = lax.axis_index("island")
    shard = lax.axis_index("shard")
    z, c = island // 2, lax.rem(island, 2)
    x, y = shard // NY, lax.rem(shard, NY)
    o = 1 - c

    def at_x(d):
        return (island, lax.rem(x + d, NX) * NY + y)

    def at_y(d):
        return (island, x * NY + lax.rem(y + d, NY))

    def at_z(d):
        return (lax.rem(z + d, NZ) * 2 + c, shard)

    sibling = (z * 2 + o, shard)
    def send(src, dst, s, r, device):
        pltpu.make_async_remote_copy(
            src_ref=src, dst_ref=dst, send_sem=s, recv_sem=r, device_id=device, device_id_type=MESH
        ).start()

    def whole_copy(whole, sem):
        return pltpu.make_async_remote_copy(
            src_ref=whole, dst_ref=whole, send_sem=sem, recv_sem=sem, device_id=sibling, device_id_type=MESH
        )

    def arrive(whole, r):
        whole_copy(whole, r).wait_recv()

    def sent(whole, s):
        whole_copy(whole, s).wait_send()

    barrier = pltpu.get_barrier_semaphore()
    partners = [at_y(d) for d in range(1, NY)] + [at_z(d) for d in range(1, NZ)] + [at_x(d) for d in range(1, NX)]
    for device in partners + [sibling]:
        pl.semaphore_signal(barrier, inc=1, device_id=device, device_id_type=MESH)

    basis_load = pltpu.make_async_copy(basis, basis_v, basis_sem)
    basis_load.start()
    for b in range(NZ):
        cols = pl.ds(pl.multiple_of((2 * b + c) * BLOCK, BLOCK), BLOCK)
        pltpu.make_async_copy(deltas.at[0, :, cols], d_own.at[:, pl.ds(b * BLOCK, BLOCK)], load_sem).start()

    basis_load.wait()
    pl.semaphore_wait(barrier, len(partners) + 1)

    mine = lax.rem(y // 2, 2) == c
    own_slot = 4 * x + 2 * (y // 4) + lax.rem(y, 2)

    def slot(index):
        return s_all.at[pl.ds(pl.multiple_of(index * SHARD, SHARD), SHARD)]

    @pl.when(mine)
    def _():
        for d in (1, 7, 4, 2, 6, 3, 5):
            for t in range(2):
                here = slot(own_slot).at[pl.ds(SHARD // 2 * t, SHARD // 2)]
                send(basis_v.at[pl.ds(SHARD // 2 * t, SHARD // 2)], here, sy_s, sy_r.at[own_slot - 4 * x, t], at_y(d))
        slot(own_slot)[...] = basis_v[...]

    for b in range(NZ):
        cols = pl.ds(pl.multiple_of((2 * b + o) * BLOCK, BLOCK), BLOCK)
        send(deltas.at[0, :, cols], d_sib.at[:, pl.ds(b * BLOCK, BLOCK)], ds_s, ds_r, sibling)

    turn = 1 - 2 * lax.rem(y, 2)
    order = [jnp.where(mine, a, b) * turn for a, b in ((0, -1), (1, 2), (-3, -2), (4, 3))]
    for n, offset in enumerate(order):
        source = lax.rem(y + offset + NY, NY)
        k = lax.rem(source, 2) + 2 * (source // 4)
        for t in range(2):
            here = slot(4 * x + k).at[pl.ds(SHARD // 2 * t, SHARD // 2)]
            if n == 0:

                @pl.when(jnp.logical_not(mine))
                def _():
                    arrive(here, sy_r.at[k, t])
            else:
                arrive(here, sy_r.at[k, t])
            for d in AROUND_4:
                send(here, here, sx_s, sx_r.at[d - 1], at_x(d))

    pltpu.make_async_copy(d_own, d_own, load_sem).wait()
    arrive(d_sib, ds_r)

    def quarter(d):
        return pl.ds(pl.multiple_of(4 * SHARD * lax.rem(x + NX - d, NX), 4 * SHARD), 4 * SHARD)

    def left_term(d):
        cols = quarter(d)
        return dot(d_own[:, cols], s_all[cols, :]) + dot(d_sib[:, cols], s_all[cols, :])

    l_part[...] = left_term(0)
    for d in (1, 3, 2):
        arrive(s_all.at[quarter(d)], sx_r.at[d - 1])
        l_part[...] += left_term(d)
    send(l_part.at[pl.ds(pl.multiple_of(HALF * o, HALF), HALF)], l_sib, lc_s, lc_r, sibling)
    arrive(l_sib, lc_r)
    l_half[...] = l_part[pl.ds(pl.multiple_of(HALF * c, HALF), HALF), :] + l_sib[...]
    for d in AROUND_8:
        rows = pl.ds(pl.multiple_of(PIECE * lax.rem(z + d, NZ), 8), PIECE)
        send(l_half.at[rows], l_in.at[d], lz_s, lz_r, at_z(d))
    total = l_half[pl.ds(pl.multiple_of(PIECE * z, 8), PIECE), :]
    arrive(l_in.at[pl.ds(1, NZ - 1)], lz_r)
    for d in range(1, NZ):
        total = total + l_in[d]

    own_half = l_all.at[pl.ds(pl.multiple_of(HALF * c, HALF), HALF)]
    piece = l_all.at[pl.ds(pl.multiple_of(HALF * c + PIECE * z, 8), PIECE)]
    piece[...] = total
    others = l_half.at[pl.ds(0, HALF - PIECE)]
    for d in AROUND_8:
        send(piece, piece, la_s, la_r, at_z(d))
    arrive(others, la_r)
    send(own_half, own_half, lf_s, lf_r, sibling)
    arrive(l_half, lf_r)

    left = l_all[...]
    left_t = left.T

    g_own[...] = dot(jnp.where(c == 0, left_t[: RANK // 2], left_t[RANK // 2 :]), left, HIGHEST)
    first, second = pl.ds(0, RANK // 4), pl.ds(RANK // 4, RANK // 4)
    for d in AROUND_8:
        send(g_own.at[first], g_yin.at[0, d], gy_s, gy_r.at[0], at_y(d))
    for d in AROUND_4:
        send(g_own.at[second], g_xin.at[1, d], gx_s, gx_r.at[1], at_x(d))

    high = left_t.astype(BF16)
    low = (left_t - high.astype(F32)).astype(BF16)
    both = jnp.concatenate([high, low], axis=0)

    def rank_of(d):
        return pl.ds(pl.multiple_of(SLICE * lax.rem(x + d, NX), SLICE), SLICE)

    def send_b(n, q):
        send(b_b16.at[q, n], b_zin.at[q, n], bz_s, bz_r.at[q], at_z(AROUND_8[n]))

    for n, away in enumerate((*AROUND_8, 0)):
        cols = pl.ds(pl.multiple_of(BLOCK * lax.rem(z + away, NZ), BLOCK), BLOCK)
        term = dot(both, d_own[:, cols]) + dot(both, d_sib[:, cols])
        term = term[:RANK] + term[RANK:]
        a_f32[n] = term[:, :RANK]
        a_b16[n] = term[:, :RANK].astype(BF16)
        for q in range(2):
            for i in range(NX):
                rows = slice(SLICE * i + PART * q, SLICE * i + PART * (q + 1))
                if away:
                    b_b16[q, n, i] = term[rows, RANK:].astype(BF16)
                else:
                    b_f32[q, i] = term[rows, RANK:]
        if away:
            send_b(n, 0)
        if n % 4 == 3:
            h = n // 4
            part = pl.ds(4 * h, 4)
            for d in AROUND_4:
                send(a_b16.at[part, rank_of(d)], a_x.at[d, part], ax_s, ax_r.at[h], at_x(d))
    for n in range(NZ - 1):
        send_b(n, 1)

    others_x, others_y, others_z = pl.ds(1, NX - 1), pl.ds(1, NY - 1), pl.ds(0, NZ - 1)
    arrive(g_xin.at[1, others_x], gx_r.at[1])
    g_second = g_own[second, :]
    for d in range(1, NX):
        g_second = g_second + g_xin[1, d]
    g_sum[1] = g_second
    for d in AROUND_8:
        send(g_sum.at[1], g_yin.at[1, d], gy_s, gy_r.at[1], at_y(d))

    def send_a(n, q):
        send(a_z.at[q, n], a_zin.at[q, n], az_s, az_r.at[q], at_z(AROUND_8[n]))

    for h in range(2):
        arrive(a_x.at[others_x, pl.ds(4 * h, 4)], ax_r.at[h])
        for n in range(4 * h, 4 * h + 4):
            term = a_f32[n, rank_of(0), :]
            for d in range(1, NX):
                term = term + a_x[d, n].astype(F32)
            a_z[0, n] = term[:PART]
            a_z[1, n] = term[PART:]
            if n < NZ - 1:
                send_a(n, 0)
    for n in range(NZ - 1):
        send_a(n, 1)

    def sum_b(q):
        arrive(b_zin.at[q, others_z], bz_r.at[q])
        total = b_f32[q]
        for n in range(NZ - 1):
            total = total + b_zin[q, n].astype(F32)
        b_x[q] = total
        for d in AROUND_4:
            send(b_x.at[q, lax.rem(x + d, NX)], b_xin.at[q, d], bx_s, bx_r.at[q], at_x(d))

    def send_y(u):
        for d in AROUND_8:
            send(r_y.at[u], r_yin.at[u, d], ry_s, ry_r.at[u], at_y(d))

    def end_a(q):
        arrive(a_zin.at[q, others_z], az_r.at[q])
        total = a_z[q, NZ - 1]
        for n in range(NZ - 1):
            total = total + a_zin[q, n]
        r_y[q] = total
        send_y(q)

    def end_b(q):
        arrive(b_xin.at[q, others_x], bx_r.at[q])
        total = b_x[q, x]
        for d in range(1, NX):
            total = total + b_xin[q, d]
        r_y[2 + q] = total
        send_y(2 + q)

    sum_b(0)
    arrive(g_yin.at[0, others_y], gy_r.at[0])
    g_first = g_own[first, :]
    for d in range(1, NY):
        g_first = g_first + g_yin[0, d]
    g_sum[0] = g_first
    for d in AROUND_4:
        send(g_sum.at[0], g_xin.at[0, d], gx_s, gx_r.at[0], at_x(d))
    sum_b(1)
    end_b(0)
    end_a(0)
    arrive(g_xin.at[0, others_x], gx_r.at[0])
    for d in range(1, NX):
        g_first = g_first + g_xin[0, d]
    arrive(g_yin.at[1, others_y], gy_r.at[1])
    for d in range(1, NY):
        g_second = g_second + g_yin[1, d]
    rows_c = pl.ds(pl.multiple_of(RANK // 2 * c, RANK // 2), RANK // 2)
    rows_o = pl.ds(pl.multiple_of(RANK // 2 * o, RANK // 2), RANK // 2)
    g_all[rows_c, :] = jnp.concatenate([g_first, g_second], axis=0)
    send(g_all.at[rows_c], g_all.at[rows_c], gc_s, gc_r, sibling)
    end_a(1)
    end_b(1)

    arrive(g_all.at[rows_o], gc_r)
    inverse = invert_steps(g_all[...], 16)

    for u in (2, 0, 1, 3):
        arrive(r_yin.at[u, others_y], ry_r.at[u])
        total = r_y[u]
        for d in range(1, NY):
            total = total + r_yin[u, d]
        here = r_all.at[u // 2, pl.ds(pl.multiple_of(SLICE * x + PART * (u % 2), PART), PART)]
        here[...] = total
        for d in AROUND_4:
            send(here, here, ra_s, ra_r, at_x(d))
    ortho_out[...] = dot(l_all[...], inverse, HIGHEST) * (1.0 / 16.0)

    @pl.when(mine)
    def _():
        sent(s_all.at[pl.ds(0, (NY - 1) * SHARD)], sy_s)

    sent(d_sib, ds_s)
    sent(s_all.at[pl.ds(0, 4 * (NX - 1) * SHARD)], sx_s)
    sent(l_half, lc_s)
    sent(others, lz_s)
    sent(others, la_s)
    sent(l_half, lf_s)
    sent(a_b16.at[pl.ds(0, 2 * (NX - 1))], ax_s)
    sent(a_z.at[:, others_z], az_s)
    sent(b_b16.at[:, others_z], bz_s)
    sent(b_x.at[:, others_x], bx_s)
    sent(r_yin.at[:, others_y], ry_s)
    sent(g_yin.at[:, others_y], gy_s)
    sent(g_xin.at[:, others_x], gx_s)
    sent(g_own, gc_s)
    right_others = r_yin.at[:, others_x]
    arrive(right_others, ra_r)
    sent(right_others, ra_s)


def update(ortho, right, params, momentum, new_params, new_momentum, p_v, m_v, sem):
    stores = []
    for n in range(ROWS // STRIP):
        rows = slice(n * STRIP, (n + 1) * STRIP)
        for h in range(2):
            cols = slice(h * RANK, (h + 1) * RANK)
            grad = dot(ortho[rows, :], right[h], HIGHEST)
            updated = outer_decay * momentum[rows, cols] + grad
            m_v[rows, cols] = updated
            p_v[rows, cols] = params[rows, cols] - outer_rate * (grad + outer_decay * updated)
        for k, (src, dst) in enumerate(((m_v, new_momentum), (p_v, new_params))):
            copy = pltpu.make_async_copy(src.at[rows], dst.at[rows], sem.at[n, k])
            copy.start()
            stores.append(copy)
    for copy in stores:
        copy.wait()


def body(island_deltas, start_basis, outer_params, momentum):
    dma = pltpu.SemaphoreType.DMA
    vmem = pltpu.VMEM
    scratch = [
        vmem((SHARD, RANK), BF16),
        vmem((ROWS, NZ * BLOCK), BF16),
        vmem((ROWS, NZ * BLOCK), BF16),
        vmem((NZ * BLOCK, RANK), BF16),
        vmem((ROWS, RANK), F32),
        vmem((HALF, RANK), F32),
        vmem((HALF, RANK), F32),
        vmem((NZ, PIECE, RANK), F32),
        vmem((ROWS, RANK), F32),
        vmem((NZ, RANK, RANK), F32),
        vmem((NZ, RANK, RANK), BF16),
        vmem((NX, NZ, SLICE, RANK), BF16),
        vmem((2, NZ, PART, RANK), F32),
        vmem((2, NZ, PART, RANK), F32),
        vmem((2, NX, PART, RANK), F32),
        vmem((2, NZ, NX, PART, RANK), BF16),
        vmem((2, NZ, NX, PART, RANK), BF16),
        vmem((2, NX, PART, RANK), F32),
        vmem((2, NX, PART, RANK), F32),
        vmem((4, PART, RANK), F32),
        vmem((4, NY, PART, RANK), F32),
        vmem((RANK // 2, RANK), F32),
        vmem((2, NY, RANK // 4, RANK), F32),
        vmem((2, NX, RANK // 4, RANK), F32),
        vmem((2, RANK // 4, RANK), F32),
        vmem((RANK, RANK), F32),
        *[dma(())] * 2,
        *[dma(())] * 2,
        dma(()),
        dma((4, 2)),
        dma(()),
        dma((NX - 1,)),
        *[dma(())] * 8,
        dma(()),
        dma((2,)),
        *[dma(()), dma((2,))] * 3,
        *[dma(()), dma((4,))],
        *[dma(())] * 2,
        *[dma(()), dma((2,))] * 2,
        *[dma(())] * 2,
    ]
    in_vmem = pl.BlockSpec(memory_space=pltpu.VMEM)
    ortho, right = pl.pallas_call(
        kernel,
        name="factors",
        out_shape=(jax.ShapeDtypeStruct((ROWS, RANK), F32), jax.ShapeDtypeStruct((2, RANK, RANK), F32)),
        in_specs=[pl.BlockSpec(memory_space=pl.ANY)] * 2,
        out_specs=(in_vmem, in_vmem),
        scratch_shapes=scratch,
        compiler_params=pltpu.CompilerParams(
            collective_id=0, has_side_effects=True, vmem_limit_bytes=24 * 1024 * 1024
        ),
    )(
        pltpu.with_memory_space_constraint(island_deltas, pltpu.HBM),
        pltpu.with_memory_space_constraint(start_basis, pltpu.HBM),
    )
    state = jax.ShapeDtypeStruct(outer_params.shape, F32)
    return tuple(
        pl.pallas_call(
            update,
            name="update",
            out_shape=(state, state),
            in_specs=[in_vmem] * 4,
            out_specs=(pl.BlockSpec(memory_space=pl.ANY),) * 2,
            scratch_shapes=[vmem((ROWS, BLOCK), F32), vmem((ROWS, BLOCK), F32), dma((ROWS // STRIP, 2))],
            compiler_params=pltpu.CompilerParams(vmem_limit_bytes=8 * 1024 * 1024),
        )(ortho, right, outer_params, momentum)
    )


def solution(mesh):
    placed = (
        P("island", "shard", None),
        P("shard", None),
        P("shard", "island"),
        P("shard", "island"),
    )
    return jax.shard_map(
        body,
        mesh=mesh,
        in_specs=placed,
        out_specs=(P("shard", "island"), P("shard", "island")),
        check_vma=False,
    )
```

```python
import functools

import jax
import jax.numpy as jnp
from jax import lax
from jax.experimental import pallas as pl
from jax.experimental.pallas import tpu as pltpu
from jax.sharding import PartitionSpec as P

outer_rate = 0.7
outer_decay = 0.9

MESH = pl.DeviceIdType.MESH
F32 = jnp.float32
BF16 = jnp.bfloat16
HIGHEST = lax.Precision.HIGHEST

NX, NY, NZ = 4, 8, 8
ROWS = 384
RANK = 128
HALF = ROWS // 2
STRIP = ROWS // 3
PIECE = HALF // NZ
BLOCK = 256
SHARD = 128
SLICE = RANK // NX
PART = SLICE // 2


AROUND_8 = (4, 3, 5, 2, 6, 1, 7)
AROUND_4 = (1, 3, 2)


def dot(a, b, precision=None):
    return jnp.dot(a, b, preferred_element_type=F32, precision=precision)


def invert_steps(a, steps):
    lane = lax.broadcasted_iota(jnp.int32, (8, RANK), 1)
    row = lax.broadcasted_iota(jnp.int32, (8, RANK), 0)

    def step(_, a):
        panel = a[0:8, :]
        columns = [jnp.broadcast_to(panel[:, j : j + 1], (8, RANK)) for j in range(8)]
        panel = jnp.where(lane < 8, (lane == row).astype(F32), panel)
        for j in range(8):
            here = row == j
            pivot = 1.0 / jnp.broadcast_to(columns[j][j : j + 1, :], (8, RANK))

            def reduced(values, j=j, here=here, pivot=pivot):
                scaled = jnp.broadcast_to(values[j : j + 1, :], (8, RANK)) * pivot
                return jnp.where(here, scaled, values - columns[j] * scaled)

            panel = reduced(panel)
            for m in range(j + 1, 8):
                columns[m] = reduced(columns[m])
        rest = a[8:, :]
        kept = jnp.where(lax.broadcasted_iota(jnp.int32, rest.shape, 1) < 8, 0.0, rest)
        for j in range(8):
            kept = kept - jnp.broadcast_to(rest[:, j : j + 1], rest.shape) * jnp.broadcast_to(
                panel[j : j + 1, :], rest.shape
            )
        return pltpu.roll(jnp.concatenate([kept, panel], axis=0), RANK - 8, 1)

    return lax.fori_loop(0, steps, step, a)


def kernel(
    deltas, basis, ortho_out, r_all,
    basis_v, d_own, d_sib, s_all, l_part, l_sib, l_half, l_in, l_all,
    a_f32, a_b16, a_x, a_z, a_zin, b_f32, b_b16, b_zin, b_x, b_xin, r_y, r_yin,
    g_own, g_yin, g_xin, g_sum, g_all,
    load_sem, basis_sem,
    ds_s, ds_r, sy_s, sy_r, sx_s, sx_r, lc_s, lc_r, lz_s, lz_r, la_s, la_r, lf_s, lf_r,
    ax_s, ax_r, az_s, az_r, bz_s, bz_r, bx_s, bx_r, ry_s, ry_r, ra_s, ra_r, gy_s, gy_r, gx_s, gx_r, gc_s, gc_r,
):
    island = lax.axis_index("island")
    shard = lax.axis_index("shard")
    z, c = island // 2, lax.rem(island, 2)
    x, y = shard // NY, lax.rem(shard, NY)
    o = 1 - c

    def at_x(d):
        return (island, lax.rem(x + d, NX) * NY + y)

    def at_y(d):
        return (island, x * NY + lax.rem(y + d, NY))

    def at_z(d):
        return (lax.rem(z + d, NZ) * 2 + c, shard)

    sibling = (z * 2 + o, shard)
    def send(src, dst, s, r, device):
        pltpu.make_async_remote_copy(
            src_ref=src, dst_ref=dst, send_sem=s, recv_sem=r, device_id=device, device_id_type=MESH
        ).start()

    def whole_copy(whole, sem):
        return pltpu.make_async_remote_copy(
            src_ref=whole, dst_ref=whole, send_sem=sem, recv_sem=sem, device_id=sibling, device_id_type=MESH
        )

    def arrive(whole, r):
        whole_copy(whole, r).wait_recv()

    def sent(whole, s):
        whole_copy(whole, s).wait_send()

    barrier = pltpu.get_barrier_semaphore()
    partners = [at_y(d) for d in range(1, NY)] + [at_z(d) for d in range(1, NZ)] + [at_x(d) for d in range(1, NX)]
    for device in partners + [sibling]:
        pl.semaphore_signal(barrier, inc=1, device_id=device, device_id_type=MESH)

    basis_load = pltpu.make_async_copy(basis, basis_v, basis_sem)
    basis_load.start()
    for b in range(NZ):
        cols = pl.ds(pl.multiple_of((2 * b + c) * BLOCK, BLOCK), BLOCK)
        pltpu.make_async_copy(deltas.at[0, :, cols], d_own.at[:, pl.ds(b * BLOCK, BLOCK)], load_sem).start()

    basis_load.wait()
    pl.semaphore_wait(barrier, len(partners) + 1)

    mine = lax.rem(y // 2, 2) == c
    own_slot = 4 * x + 2 * (y // 4) + lax.rem(y, 2)

    def slot(index):
        return s_all.at[pl.ds(pl.multiple_of(index * SHARD, SHARD), SHARD)]

    @pl.when(mine)
    def _():
        for d in (1, 7, 4, 2, 6, 3, 5):
            for t in range(2):
                here = slot(own_slot).at[pl.ds(SHARD // 2 * t, SHARD // 2)]
                send(basis_v.at[pl.ds(SHARD // 2 * t, SHARD // 2)], here, sy_s, sy_r.at[own_slot - 4 * x, t], at_y(d))
        slot(own_slot)[...] = basis_v[...]

    for b in range(NZ):
        cols = pl.ds(pl.multiple_of((2 * b + o) * BLOCK, BLOCK), BLOCK)
        send(deltas.at[0, :, cols], d_sib.at[:, pl.ds(b * BLOCK, BLOCK)], ds_s, ds_r, sibling)

    turn = 1 - 2 * lax.rem(y, 2)
    order = [jnp.where(mine, a, b) * turn for a, b in ((0, -1), (1, 2), (-3, -2), (4, 3))]
    for n, offset in enumerate(order):
        source = lax.rem(y + offset + NY, NY)
        k = lax.rem(source, 2) + 2 * (source // 4)
        for t in range(2):
            here = slot(4 * x + k).at[pl.ds(SHARD // 2 * t, SHARD // 2)]
            if n == 0:

                @pl.when(jnp.logical_not(mine))
                def _():
                    arrive(here, sy_r.at[k, t])
            else:
                arrive(here, sy_r.at[k, t])
            for d in AROUND_4:
                send(here, here, sx_s, sx_r.at[d - 1], at_x(d))

    pltpu.make_async_copy(d_own, d_own, load_sem).wait()
    arrive(d_sib, ds_r)

    def quarter(d):
        return pl.ds(pl.multiple_of(4 * SHARD * lax.rem(x + NX - d, NX), 4 * SHARD), 4 * SHARD)

    def left_term(d):
        cols = quarter(d)
        return dot(d_own[:, cols], s_all[cols, :]) + dot(d_sib[:, cols], s_all[cols, :])

    l_part[...] = left_term(0)
    for d in (1, 3, 2):
        arrive(s_all.at[quarter(d)], sx_r.at[d - 1])
        l_part[...] += left_term(d)
    send(l_part.at[pl.ds(pl.multiple_of(HALF * o, HALF), HALF)], l_sib, lc_s, lc_r, sibling)
    arrive(l_sib, lc_r)
    l_half[...] = l_part[pl.ds(pl.multiple_of(HALF * c, HALF), HALF), :] + l_sib[...]
    for d in AROUND_8:
        rows = pl.ds(pl.multiple_of(PIECE * lax.rem(z + d, NZ), 8), PIECE)
        send(l_half.at[rows], l_in.at[d], lz_s, lz_r, at_z(d))
    total = l_half[pl.ds(pl.multiple_of(PIECE * z, 8), PIECE), :]
    arrive(l_in.at[pl.ds(1, NZ - 1)], lz_r)
    for d in range(1, NZ):
        total = total + l_in[d]

    own_half = l_all.at[pl.ds(pl.multiple_of(HALF * c, HALF), HALF)]
    piece = l_all.at[pl.ds(pl.multiple_of(HALF * c + PIECE * z, 8), PIECE)]
    piece[...] = total
    others = l_half.at[pl.ds(0, HALF - PIECE)]
    for d in AROUND_8:
        send(piece, piece, la_s, la_r, at_z(d))
    arrive(others, la_r)
    send(own_half, own_half, lf_s, lf_r, sibling)
    arrive(l_half, lf_r)

    left = l_all[...]
    left_t = left.T

    g_own[...] = dot(jnp.where(c == 0, left_t[: RANK // 2], left_t[RANK // 2 :]), left, HIGHEST)
    first, second = pl.ds(0, RANK // 4), pl.ds(RANK // 4, RANK // 4)
    for d in AROUND_8:
        send(g_own.at[first], g_yin.at[0, d], gy_s, gy_r.at[0], at_y(d))
    for d in AROUND_4:
        send(g_own.at[second], g_xin.at[1, d], gx_s, gx_r.at[1], at_x(d))

    high = left_t.astype(BF16)
    low = (left_t - high.astype(F32)).astype(BF16)
    both = jnp.concatenate([high, low], axis=0)

    def rank_of(d):
        return pl.ds(pl.multiple_of(SLICE * lax.rem(x + d, NX), SLICE), SLICE)

    def send_b(n, q):
        send(b_b16.at[q, n], b_zin.at[q, n], bz_s, bz_r.at[q], at_z(AROUND_8[n]))

    for n, away in enumerate((*AROUND_8, 0)):
        cols = pl.ds(pl.multiple_of(BLOCK * lax.rem(z + away, NZ), BLOCK), BLOCK)
        term = dot(both, d_own[:, cols]) + dot(both, d_sib[:, cols])
        term = term[:RANK] + term[RANK:]
        a_f32[n] = term[:, :RANK]
        a_b16[n] = term[:, :RANK].astype(BF16)
        for q in range(2):
            for i in range(NX):
                rows = slice(SLICE * i + PART * q, SLICE * i + PART * (q + 1))
                if away:
                    b_b16[q, n, i] = term[rows, RANK:].astype(BF16)
                else:
                    b_f32[q, i] = term[rows, RANK:]
        if away:
            send_b(n, 0)
        if n % 4 == 3:
            h = n // 4
            part = pl.ds(4 * h, 4)
            for d in AROUND_4:
                send(a_b16.at[part, rank_of(d)], a_x.at[d, part], ax_s, ax_r.at[h], at_x(d))
    for n in range(NZ - 1):
        send_b(n, 1)

    others_x, others_y, others_z = pl.ds(1, NX - 1), pl.ds(1, NY - 1), pl.ds(0, NZ - 1)
    arrive(g_xin.at[1, others_x], gx_r.at[1])
    g_second = g_own[second, :]
    for d in range(1, NX):
        g_second = g_second + g_xin[1, d]
    g_sum[1] = g_second
    for d in AROUND_8:
        send(g_sum.at[1], g_yin.at[1, d], gy_s, gy_r.at[1], at_y(d))

    def send_a(n, q):
        send(a_z.at[q, n], a_zin.at[q, n], az_s, az_r.at[q], at_z(AROUND_8[n]))

    for h in range(2):
        arrive(a_x.at[others_x, pl.ds(4 * h, 4)], ax_r.at[h])
        for n in range(4 * h, 4 * h + 4):
            term = a_f32[n, rank_of(0), :]
            for d in range(1, NX):
                term = term + a_x[d, n].astype(F32)
            a_z[0, n] = term[:PART]
            a_z[1, n] = term[PART:]
            if n < NZ - 1:
                send_a(n, 0)
    for n in range(NZ - 1):
        send_a(n, 1)

    def sum_b(q):
        arrive(b_zin.at[q, others_z], bz_r.at[q])
        total = b_f32[q]
        for n in range(NZ - 1):
            total = total + b_zin[q, n].astype(F32)
        b_x[q] = total
        for d in AROUND_4:
            send(b_x.at[q, lax.rem(x + d, NX)], b_xin.at[q, d], bx_s, bx_r.at[q], at_x(d))

    def send_y(u):
        for d in AROUND_8:
            send(r_y.at[u], r_yin.at[u, d], ry_s, ry_r.at[u], at_y(d))

    def end_a(q):
        arrive(a_zin.at[q, others_z], az_r.at[q])
        total = a_z[q, NZ - 1]
        for n in range(NZ - 1):
            total = total + a_zin[q, n]
        r_y[q] = total
        if q == 1:
            both_q = pl.ds(0, 2)
            for d in AROUND_8:
                send(r_y.at[both_q], r_yin.at[both_q, d], ry_s, ry_r.at[0], at_y(d))

    def end_b(q):
        arrive(b_xin.at[q, others_x], bx_r.at[q])
        total = b_x[q, x]
        for d in range(1, NX):
            total = total + b_xin[q, d]
        r_y[2 + q] = total
        send_y(2 + q)

    sum_b(0)
    arrive(g_yin.at[0, others_y], gy_r.at[0])
    g_first = g_own[first, :]
    for d in range(1, NY):
        g_first = g_first + g_yin[0, d]
    g_sum[0] = g_first
    for d in AROUND_4:
        send(g_sum.at[0], g_xin.at[0, d], gx_s, gx_r.at[0], at_x(d))
    sum_b(1)
    end_b(0)
    end_a(0)
    arrive(g_xin.at[0, others_x], gx_r.at[0])
    for d in range(1, NX):
        g_first = g_first + g_xin[0, d]
    arrive(g_yin.at[1, others_y], gy_r.at[1])
    for d in range(1, NY):
        g_second = g_second + g_yin[1, d]
    rows_c = pl.ds(pl.multiple_of(RANK // 2 * c, RANK // 2), RANK // 2)
    rows_o = pl.ds(pl.multiple_of(RANK // 2 * o, RANK // 2), RANK // 2)
    g_all[rows_c, :] = jnp.concatenate([g_first, g_second], axis=0)
    send(g_all.at[rows_c], g_all.at[rows_c], gc_s, gc_r, sibling)
    end_a(1)
    end_b(1)

    arrive(g_all.at[rows_o], gc_r)
    inverse = invert_steps(g_all[...], 16)

    for u in (2, 0, 1, 3):
        if u == 0:
            arrive(r_yin.at[pl.ds(0, 2), others_y], ry_r.at[0])
        elif u > 1:
            arrive(r_yin.at[u, others_y], ry_r.at[u])
        total = r_y[u]
        for d in range(1, NY):
            total = total + r_yin[u, d]
        here = r_all.at[u // 2, pl.ds(pl.multiple_of(SLICE * x + PART * (u % 2), PART), PART)]
        here[...] = total
        for d in AROUND_4:
            send(here, here, ra_s, ra_r, at_x(d))
    ortho_out[...] = dot(l_all[...], inverse, HIGHEST) * (1.0 / 16.0)

    @pl.when(mine)
    def _():
        sent(s_all.at[pl.ds(0, (NY - 1) * SHARD)], sy_s)

    sent(d_sib, ds_s)
    sent(s_all.at[pl.ds(0, 4 * (NX - 1) * SHARD)], sx_s)
    sent(l_half, lc_s)
    sent(others, lz_s)
    sent(others, la_s)
    sent(l_half, lf_s)
    sent(a_b16.at[pl.ds(0, 2 * (NX - 1))], ax_s)
    sent(a_z.at[:, others_z], az_s)
    sent(b_b16.at[:, others_z], bz_s)
    sent(b_x.at[:, others_x], bx_s)
    sent(r_yin.at[:, others_y], ry_s)
    sent(g_yin.at[:, others_y], gy_s)
    sent(g_xin.at[:, others_x], gx_s)
    sent(g_own, gc_s)
    right_others = r_yin.at[:, others_x]
    arrive(right_others, ra_r)
    sent(right_others, ra_s)


def update(ortho, right, params, momentum, new_params, new_momentum, p_v, m_v, sem):
    stores = []
    for n in range(ROWS // STRIP):
        rows = slice(n * STRIP, (n + 1) * STRIP)
        for h in range(2):
            cols = slice(h * RANK, (h + 1) * RANK)
            grad = dot(ortho[rows, :], right[h], HIGHEST)
            updated = outer_decay * momentum[rows, cols] + grad
            m_v[rows, cols] = updated
            p_v[rows, cols] = params[rows, cols] - outer_rate * (grad + outer_decay * updated)
        for k, (src, dst) in enumerate(((m_v, new_momentum), (p_v, new_params))):
            copy = pltpu.make_async_copy(src.at[rows], dst.at[rows], sem.at[n, k])
            copy.start()
            stores.append(copy)
    for copy in stores:
        copy.wait()


def body(island_deltas, start_basis, outer_params, momentum):
    dma = pltpu.SemaphoreType.DMA
    vmem = pltpu.VMEM
    scratch = [
        vmem((SHARD, RANK), BF16),
        vmem((ROWS, NZ * BLOCK), BF16),
        vmem((ROWS, NZ * BLOCK), BF16),
        vmem((NZ * BLOCK, RANK), BF16),
        vmem((ROWS, RANK), F32),
        vmem((HALF, RANK), F32),
        vmem((HALF, RANK), F32),
        vmem((NZ, PIECE, RANK), F32),
        vmem((ROWS, RANK), F32),
        vmem((NZ, RANK, RANK), F32),
        vmem((NZ, RANK, RANK), BF16),
        vmem((NX, NZ, SLICE, RANK), BF16),
        vmem((2, NZ, PART, RANK), F32),
        vmem((2, NZ, PART, RANK), F32),
        vmem((2, NX, PART, RANK), F32),
        vmem((2, NZ, NX, PART, RANK), BF16),
        vmem((2, NZ, NX, PART, RANK), BF16),
        vmem((2, NX, PART, RANK), F32),
        vmem((2, NX, PART, RANK), F32),
        vmem((4, PART, RANK), F32),
        vmem((4, NY, PART, RANK), F32),
        vmem((RANK // 2, RANK), F32),
        vmem((2, NY, RANK // 4, RANK), F32),
        vmem((2, NX, RANK // 4, RANK), F32),
        vmem((2, RANK // 4, RANK), F32),
        vmem((RANK, RANK), F32),
        *[dma(())] * 2,
        *[dma(())] * 2,
        dma(()),
        dma((4, 2)),
        dma(()),
        dma((NX - 1,)),
        *[dma(())] * 8,
        dma(()),
        dma((2,)),
        *[dma(()), dma((2,))] * 3,
        *[dma(()), dma((4,))],
        *[dma(())] * 2,
        *[dma(()), dma((2,))] * 2,
        *[dma(())] * 2,
    ]
    in_vmem = pl.BlockSpec(memory_space=pltpu.VMEM)
    ortho, right = pl.pallas_call(
        kernel,
        name="factors",
        out_shape=(jax.ShapeDtypeStruct((ROWS, RANK), F32), jax.ShapeDtypeStruct((2, RANK, RANK), F32)),
        in_specs=[pl.BlockSpec(memory_space=pl.ANY)] * 2,
        out_specs=(in_vmem, in_vmem),
        scratch_shapes=scratch,
        compiler_params=pltpu.CompilerParams(
            collective_id=0, has_side_effects=True, vmem_limit_bytes=24 * 1024 * 1024
        ),
    )(
        pltpu.with_memory_space_constraint(island_deltas, pltpu.HBM),
        pltpu.with_memory_space_constraint(start_basis, pltpu.HBM),
    )
    state = jax.ShapeDtypeStruct(outer_params.shape, F32)
    return tuple(
        pl.pallas_call(
            update,
            name="update",
            out_shape=(state, state),
            in_specs=[in_vmem] * 4,
            out_specs=(pl.BlockSpec(memory_space=pl.ANY),) * 2,
            scratch_shapes=[vmem((ROWS, BLOCK), F32), vmem((ROWS, BLOCK), F32), dma((ROWS // STRIP, 2))],
            compiler_params=pltpu.CompilerParams(vmem_limit_bytes=8 * 1024 * 1024),
        )(ortho, right, outer_params, momentum)
    )


def solution(mesh):
    placed = (
        P("island", "shard", None),
        P("shard", None),
        P("shard", "island"),
        P("shard", "island"),
    )
    return jax.shard_map(
        body,
        mesh=mesh,
        in_specs=placed,
        out_specs=(P("shard", "island"), P("shard", "island")),
        check_vma=False,
    )
```
